256 devices in a mesh: seq: 32 (over x, y, core), chan: 8 (over z).
Axes of the slice: x: 4, y: 4, z: 8, core: 2. Of those that a mesh axis runs over, the one named last changes fastest.
Arguments:
- query_rows: bfloat16 [8192, 8192], P('seq', 'chan'), may hold values from -17 to 17
- key_rows: bfloat16 [8192, 8192], P('seq', 'chan'), may hold values from -6 to 6
- value_rows: bfloat16 [8192, 8192], P('seq', 'chan'), may hold values from -6 to 6
- short_taps: bfloat16 [3, 3, 8192], P(None, None, 'chan'), may hold values from -2.390625 to 2.390625
- medium_taps: bfloat16 [128, 8192], P(None, 'chan'), may hold values from -0.5 to 0.5
- residues: float32 [16, 8192], P(None, 'chan'), may hold values from -0.26 to 0.26
- decay_rates: float32 [16, 8192], P(None, 'chan'), may hold values from 3.6621094e-05 to 0.0333333333
- skip_gain: float32 [8192], P('chan'), may hold values from -3 to 3
- norm_gain: float32 [8192], P('chan'), may hold values from 0.1 to 1.9
Outputs:
- hyena_out: bfloat16 [8192, 8192], P('seq', 'chan')
The draws below stay inside these ranges and needn't reach their ends.
All inputs are finite; a program needn't handle non-finite values.
Results may differ from the reference program's by a relative error of at most 0.018.
Values may be sent and summed in bfloat16 or wider, within the bound.
A program may use at most 64 MiB of HBM per device.

```python
import math
import jax
import jax.numpy as jnp
from jax import lax

D = 8192
TAPS = 128
POLES = 16
LENGTH = 8192


def pole_rates(key, lowest, highest):
    spread = jax.random.uniform(key, (POLES, D), jnp.float32)
    return jnp.exp(math.log(lowest) + spread * (math.log(highest) - math.log(lowest)))


def draw_decay_rates(key, part):
    speed = pole_rates(key, 0.5 / LENGTH, 1.0 / 30.0)
    return speed


def draw_residues(key, part):
    speed = pole_rates(key, 0.5 / LENGTH, 1.0 / 30.0)
    key = jax.random.fold_in(key, 5)
    base = jax.random.truncated_normal(key, -4.0, 4.0, (POLES, D), jnp.float32)
    return base * jnp.sqrt(2.0 * speed / POLES)


def draw_query_rows(key, part):
    key = jax.random.fold_in(key, 11)
    first_key, second_key = jax.random.split(key)
    spread = jax.random.uniform(first_key, (1, D), jnp.float32)
    rising = jnp.arange(D).astype(jnp.float32)[None, :] / D - 0.5
    base = jax.random.truncated_normal(second_key, -4.0, 4.0, (LENGTH, D), jnp.float32)
    scale = jnp.exp(math.log(10.0) * spread - 1.15 + 0.5 * math.log(3.0) * rising)
    return (base * scale).astype(jnp.bfloat16)


def levels(rng, extent, cuts, least, top_value):
    def one(position, parts):
        steps = jax.random.uniform(jax.random.fold_in(jax.random.fold_in(rng, 6), position), (parts,), jnp.float32, least / len(cuts), top_value / len(cuts))
        return jnp.repeat(jnp.exp(steps), extent[position] // parts).reshape((-1,) + (1,) * (len(extent) - position - 1))

    gain = one(*cuts[0])
    for cut in cuts[1:]:
        gain = gain * one(*cut)
    return gain


def gaussian(own_key, dims, width, most, pieces=(), dtype=jnp.bfloat16):
    gain = levels(own_key, dims, pieces, -0.22, 0.18) if pieces else 1.0
    values = jax.random.normal(own_key, dims, jnp.float32) * width * gain
    return jnp.minimum(jnp.maximum(values, -most), most).astype(dtype)


def setup_inputs(seed: int = 0) -> dict:
    splits = jax.random.split(jax.random.key(seed), 10)
    query_rows = draw_query_rows(jax.random.fold_in(splits[9], 71), 0)
    key_rows = gaussian(splits[1], (LENGTH, D), 1.0, 6.0, ((0, 32), (1, 8)))
    value_rows = gaussian(splits[2], (LENGTH, D), 1.0, 6.0, ((0, 32), (1, 8)))
    short_taps = gaussian(splits[3], (3, 3, D), 0.6, 2.390625, ((2, 8),))
    medium_taps = gaussian(splits[4], (TAPS, D), TAPS ** -0.5, 0.5, ((1, 8),))
    residues = draw_residues(jax.random.fold_in(splits[9], 71), 0)
    decay_rates = draw_decay_rates(jax.random.fold_in(splits[9], 71), 0)
    skip_gain = gaussian(splits[7], (D,), 1.0, 3.0, ((0, 8),), jnp.float32)
    norm_gain = jnp.clip(1.0 + 0.18 * jax.random.normal(splits[8], (D,), jnp.float32), 0.1, 1.9)
    return {"query_rows": query_rows, "key_rows": key_rows, "value_rows": value_rows, "short_taps": short_taps, "medium_taps": medium_taps, "residues": residues, "decay_rates": decay_rates, "skip_gain": skip_gain, "norm_gain": norm_gain}


def short_conv(signal, tap_rows):
    values_f = jnp.pad(signal.astype(jnp.float32), ((2, 0), (0, 0)))
    weights = tap_rows.astype(jnp.float32)
    return weights[0] * values_f[2:] + weights[1] * values_f[1:-1] + weights[2] * values_f[:-2]

def causal_fft(signal, kernel):
    total = 2 * signal.shape[0]
    spectrum = jnp.fft.rfft(signal, n=total, axis=0) * jnp.fft.rfft(kernel, n=total, axis=0)
    return jnp.fft.irfft(spectrum, n=total, axis=0)[:signal.shape[0]]

def reference(query_rows, key_rows, value_rows, short_taps, medium_taps, residues, decay_rates, skip_gain, norm_gain):
    length, model_width = query_rows.shape
    group_size = 128
    block_count = model_width // group_size

    def split_blocks(array):
        return jnp.transpose(array.reshape(array.shape[0], block_count, group_size), (1, 0, 2))
    short_blocks = jnp.transpose(short_taps.reshape(3, 3, block_count, group_size), (2, 0, 1, 3))
    skip_blocks = skip_gain.reshape(block_count, group_size)

    def one_block(inputs):
        query_part, key_part, value_part, short_part, medium_part, residue_part, rate_part, skip_part = inputs
        query_tilde = short_conv(query_part, short_part[0]).astype(jnp.bfloat16)
        key_tilde = short_conv(key_part, short_part[1]).astype(jnp.bfloat16)
        value_tilde = short_conv(value_part, short_part[2]).astype(jnp.bfloat16)
        key_hat = causal_fft(key_tilde.astype(jnp.float32), medium_part.astype(jnp.float32))
        mixed_in = (key_hat * value_tilde.astype(jnp.float32)).astype(jnp.bfloat16)
        lag_pos = jnp.arange(length).astype(jnp.float32)[None, :, None]
        kernel = lax.optimization_barrier(jnp.sum(residue_part[:, None, :] * jnp.exp(-rate_part[:, None, :] * lag_pos), axis=0))
        long_out = causal_fft(mixed_in.astype(jnp.float32), kernel).astype(jnp.bfloat16)
        mixed_f = mixed_in.astype(jnp.float32)
        return query_tilde.astype(jnp.float32) * (long_out.astype(jnp.float32) + skip_part * mixed_f)
    gated = lax.map(one_block, (split_blocks(query_rows), split_blocks(key_rows), split_blocks(value_rows), short_blocks, split_blocks(medium_taps), split_blocks(residues), split_blocks(decay_rates), skip_blocks))
    mean_square = lax.optimization_barrier(jnp.sum(gated * gated, axis=(0, 2))) / model_width
    scale = lax.rsqrt(mean_square + 1e-05)
    gains = norm_gain.reshape(block_count, 1, group_size)
    result = (gated * scale[None, :, None] * gains).astype(jnp.bfloat16)
    return jnp.transpose(result, (1, 0, 2)).reshape(length, model_width)
```

```python
import functools
import math

import jax
import jax.numpy as jnp
import ml_dtypes
import numpy as np
from jax import lax
from jax.experimental import pallas as pl
from jax.experimental.pallas import tpu as pltpu
from jax.sharding import PartitionSpec as P

D = 8192
ROWS = 256
TAPS = 128
POLES = 16
LANES = 128
TILE = 256
EDGE = 16
HALF_ONE = 192
HALF_TWO = 256
MESH = pl.DeviceIdType.MESH
BF = jnp.bfloat16
F32 = jnp.float32


def split_np(table):
    high = table.astype(np.float32).astype(ml_dtypes.bfloat16)
    low = (table - high.astype(np.float64)).astype(np.float32).astype(ml_dtypes.bfloat16)
    return np.stack([high, low])


def odd_tables(half, positions):
    angle = (2.0 * math.pi / (2 * half)) * (np.arange(half) + 0.5)[:, None] * positions[None, :]
    return np.concatenate([np.cos(angle), -np.sin(angle)], 0)


def make_tables():
    one = odd_tables(HALF_ONE, np.arange(2 * HALF_ONE))
    two = odd_tables(HALF_TWO, np.arange(ROWS))
    turn = np.zeros((HALF_ONE, LANES), np.float32)
    base = (2.0 * math.pi / (2 * HALF_ONE)) * (np.arange(HALF_ONE) + 0.5)
    turn[:, 0] = np.cos(base)
    turn[:, 1] = np.cos(2 * base)
    turn[:, 2] = -np.sin(base)
    turn[:, 3] = -np.sin(2 * base)
    return (
        split_np(one),
        split_np(one[:, TAPS:].T.copy()),
        split_np(two),
        split_np(two.T.copy()),
        turn,
    )


def split(value):
    high = value.astype(BF)
    return high, (value - high.astype(F32)).astype(BF)


def mm(left, right):
    return jnp.dot(left, right, preferred_element_type=F32)


def kernel(
    dims,
    query,
    key,
    value,
    short_taps,
    medium_taps,
    residues,
    decay_rates,
    skip_gain,
    norm_gain,
    fwd_one,
    inv_one,
    fwd_two,
    inv_two,
    turn,
    out,
    key_own,
    key_halo,
    value_own,
    value_halo,
    query_own,
    query_halo,
    staged,
    value_tilde,
    query_tilde,
    tap_spec,
    key_spec,
    kernel_spec,
    long_kernel,
    powers,
    eighth,
    mixed,
    states_own,
    states_away,
    states_seen,
    chip_state,
    chips_seen,
    row_state,
    rows_seen,
    carry_own,
    carry_away,
    carry_seen,
    local_long,
    gated,
    squares,
    row_sums,
    sums_seen,
    result,
    load_sems,
    send_sems,
    recv_sems,
    store_sem,
):
    n_x, n_y, n_z, channels = dims
    half = channels // 2
    seq = lax.axis_index("seq")
    chan = lax.axis_index("chan")
    core = seq % 2
    y_pos = (seq // 2) % n_y
    x_pos = seq // (2 * n_y)
    n_seq = 2 * n_x * n_y
    right = (seq + 1) % n_seq
    left = (seq + n_seq - 1) % n_seq
    other = seq + 1 - 2 * core

    def along_y(step):
        return (x_pos * n_y + (y_pos + step) % n_y) * 2 + core

    def along_x(step):
        return (((x_pos + step) % n_x) * n_y + y_pos) * 2 + core

    loads = [
        pltpu.make_async_copy(source, target, load_sems.at[number])
        for number, (source, target) in enumerate(
            ((key, key_own), (value, value_own), (query, query_own))
        )
    ]
    for load in loads:
        load.start()

    barrier = pltpu.get_barrier_semaphore()
    seq_partners = [right, left, other]
    seq_partners += [along_y(step) for step in range(1, n_y)]
    seq_partners += [along_x(step) for step in range(1, n_x)]
    for partner in seq_partners:
        pl.semaphore_signal(barrier, inc=1, device_id={"seq": partner}, device_id_type=MESH)
    for step in range(1, n_z):
        pl.semaphore_signal(
            barrier, inc=1, device_id={"chan": (chan + step) % n_z}, device_id_type=MESH
        )
    pl.semaphore_wait(barrier, len(seq_partners) + n_z - 1)

    sent = []

    def send(source, target, where):
        number = len(sent)
        copy = pltpu.make_async_remote_copy(
            src_ref=source,
            dst_ref=target,
            send_sem=send_sems.at[number],
            recv_sem=recv_sems.at[number],
            device_id=where,
            device_id_type=MESH,
        )
        copy.start()
        sent.append(copy)
        return copy

    key_copy = send(key.at[pl.ds(ROWS - TAPS - EDGE, TAPS + EDGE), :], key_halo, {"seq": right})
    value_copy = send(value.at[pl.ds(ROWS - EDGE, EDGE), :], value_halo, {"seq": right})
    query_copy = send(query.at[pl.ds(ROWS - EDGE, EDGE), :], query_halo, {"seq": right})

    def lanes(start, size):
        return pl.ds(pl.multiple_of(start, size), size)

    sub = lax.broadcasted_iota(jnp.int32, (8, LANES), 0).astype(F32)

    def pole_powers(group, _):
        cols = lanes(group * LANES, LANES)
        start = []
        steps = []
        for pole in range(POLES):
            rate = decay_rates[pl.ds(pole, 1), cols]
            power = jnp.exp(-rate * sub)
            powers[pole, :, cols] = power
            step = jnp.broadcast_to(jnp.exp(-8.0 * rate), (8, LANES))
            eighth[pole, :, cols] = step
            start.append(residues[pl.ds(pole, 1), cols] * power)
            steps.append(step)

        def rows(number, running):
            total = functools.reduce(jnp.add, running)
            long_kernel[pl.ds(pl.multiple_of(number * 8, 8), 8), cols] = total
            return tuple(r * s for r, s in zip(running, steps))

        lax.fori_loop(0, ROWS // 8, rows, tuple(start), unroll=4)
        return 0

    lax.fori_loop(0, channels // LANES, pole_powers, 0)

    loads[0].wait()

    def before_halo(tile, _):
        cols = lanes(tile * TILE, TILE)
        taps = medium_taps[:, cols]
        spec = mm(fwd_one[0, :, :TAPS], taps) + mm(fwd_one[1, :, :TAPS], taps)
        first = short_taps[1, :, cols].astype(F32)
        s_re = first[0:1] + first[1:2] * turn[:, 0:1] + first[2:3] * turn[:, 1:2]
        s_im = first[1:2] * turn[:, 2:3] + first[2:3] * turn[:, 3:4]
        m_re, m_im = spec[:HALF_ONE], spec[HALF_ONE:]
        scale = 1.0 / HALF_ONE
        tap_spec[:HALF_ONE, cols] = (m_re * s_re - m_im * s_im) * scale
        tap_spec[HALF_ONE:, cols] = (m_re * s_im + m_im * s_re) * scale
        own = key_own[:, cols]
        key_spec[:, cols] = mm(fwd_one[0, :, TAPS:], own) + mm(fwd_one[1, :, TAPS:], own)
        high, low = split(long_kernel[:, cols])
        spec = mm(fwd_two[0], high) + mm(fwd_two[0], low) + mm(fwd_two[1], high)
        kernel_spec[:, cols] = spec * (1.0 / HALF_TWO)
        return 0

    lax.fori_loop(0, channels // TILE, before_halo, 0)

    def short_conv(source, halo, taps_row, target):
        def one(tile, _):
            cols = lanes(tile * TILE, TILE)
            staged[0:EDGE, :] = halo[:, cols].astype(F32)
            staged[EDGE:, :] = source[:, cols].astype(F32)
            weights = short_taps[taps_row, :, cols].astype(F32)
            total = (
                weights[0:1] * staged[EDGE:, :]
                + weights[1:2] * staged[EDGE - 1 : EDGE - 1 + ROWS, :]
                + weights[2:3] * staged[EDGE - 2 : EDGE - 2 + ROWS, :]
            )
            target[:, cols] = total.astype(BF)
            return 0

        lax.fori_loop(0, channels // TILE, one, 0)

    loads[1].wait()
    loads[2].wait()
    key_copy.wait_recv()
    value_copy.wait_recv()
    query_copy.wait_recv()

    @pl.when(seq == 0)
    def _():
        key_halo[...] = jnp.zeros_like(key_halo)
        value_halo[...] = jnp.zeros_like(value_halo)
        query_halo[...] = jnp.zeros_like(query_halo)

    short_conv(value_own, value_halo, 2, value_tilde)

    def medium(tile, away):
        cols = lanes(tile * TILE, TILE)
        past = key_halo[EDGE:, cols]
        spec = key_spec[:, cols] + mm(fwd_one[0, :, :TAPS], past) + mm(fwd_one[1, :, :TAPS], past)
        x_re, x_im = spec[:HALF_ONE], spec[HALF_ONE:]
        t_re, t_im = tap_spec[:HALF_ONE, cols], tap_spec[HALF_ONE:, cols]
        re_high, re_low = split(x_re * t_re - x_im * t_im)
        im_high, im_low = split(x_re * t_im + x_im * t_re)
        high = jnp.concatenate([re_high, im_high], 0)
        low = jnp.concatenate([re_low, im_low], 0)
        key_hat = mm(inv_one[0], high) + mm(inv_one[0], low) + mm(inv_one[1], high)
        last = short_taps[1, 2:3, cols].astype(F32) * medium_taps[TAPS - EDGE :, cols].astype(F32)[
            EDGE - 1 :
        ]
        ends = (
            key_halo[:EDGE, cols].astype(F32)[EDGE - 1 :]
            + key_own[ROWS - EDGE :, cols].astype(F32)[EDGE - 1 :]
        )
        row = lax.broadcasted_iota(jnp.int32, (ROWS, TILE), 0)
        key_hat = key_hat + jnp.where(row == 0, last * ends, 0.0)
        mixed[:, cols] = (key_hat * value_tilde[:, cols].astype(F32)).astype(BF)

    def end_states(group, target, target_group):
        cols = lanes(group * LANES, LANES)
        steps = [eighth[pole, :, cols] for pole in range(POLES)]

        def rows(number, running):
            block = mixed[pl.ds(pl.multiple_of(number * 16, 16), 16), cols].astype(F32)
            running = [r * s + block[:8] for r, s in zip(running, steps)]
            return tuple(r * s + block[8:] for r, s in zip(running, steps))

        empty = tuple(jnp.zeros((8, LANES), F32) for _ in range(POLES))
        running = lax.fori_loop(0, ROWS // 16, rows, empty, unroll=2)
        to = lanes(target_group * LANES, LANES)
        for pole in range(POLES):
            rate = decay_rates[pl.ds(pole, 1), cols]
            weighted = running[pole] * jnp.exp(-rate * (7.0 - sub))
            target[pl.ds(pole, 1), to] = jnp.sum(weighted, axis=0, keepdims=True)

    half_tiles = half // TILE
    half_groups = half // LANES

    def half_block(side, target):
        lax.fori_loop(0, half_tiles, lambda n, _: (medium(side * half_tiles + n, 0), 0)[1], 0)
        lax.fori_loop(
            0,
            half_groups,
            lambda n, _: (end_states(side * half_groups + n, target, n), 0)[1],
            0,
        )

    half_block(1 - core, states_away)
    states_copy = send(states_away, states_seen, {"seq": other})
    half_block(core, states_own)

    own_cols = lanes(core * half, half)
    rates = decay_rates[:, own_cols]
    block_decay = jnp.exp(-float(ROWS) * rates)
    states_copy.wait_recv()
    mine, theirs = states_own[...], states_seen[...]
    first = jnp.where(core == 0, mine, theirs)
    second = jnp.where(core == 0, theirs, mine)
    chip_state[...] = block_decay * first + second
    y_copies = [
        send(chip_state, chips_seen.at[step - 1], {"seq": along_y(step)}) for step in range(1, n_y)
    ]

    def long_local(tile, _):
        cols = lanes(tile * TILE, TILE)
        signal = mixed[:, cols]
        spec = mm(fwd_two[0], signal) + mm(fwd_two[1], signal)
        x_re, x_im = spec[:HALF_TWO], spec[HALF_TWO:]
        k_re, k_im = kernel_spec[:HALF_TWO, cols], kernel_spec[HALF_TWO:, cols]
        re_high, re_low = split(x_re * k_re - x_im * k_im)
        im_high, im_low = split(x_re * k_im + x_im * k_re)
        high = jnp.concatenate([re_high, im_high], 0)
        low = jnp.concatenate([re_low, im_low], 0)
        local_long[:, cols] = mm(inv_two[0], high) + mm(inv_two[0], low) + mm(inv_two[1], high)
        return 0

    tiles = channels // TILE
    lax.fori_loop(0, tiles // 2, long_local, 0)

    chip_span = float(2 * ROWS)
    row_span = float(2 * ROWS * n_y)
    y_far = (n_y - 1 - y_pos).astype(F32)
    row_total = jnp.exp(-rates * (chip_span * y_far)) * chip_state[...]
    before = jnp.zeros((POLES, half), F32)
    for step in range(1, n_y):
        y_copies[step - 1].wait_recv()
        seen = chips_seen[step - 1]
        source = (y_pos - step + n_y) % n_y
        distance = (n_y - 1 - source).astype(F32)
        row_total += jnp.exp(-rates * (chip_span * distance)) * seen
        before += jnp.where(y_pos >= step, jnp.exp(-rates * (chip_span * (step - 1))) * seen, 0.0)
    row_state[...] = row_total
    x_copies = [
        send(row_state, rows_seen.at[step - 1], {"seq": along_x(step)}) for step in range(1, n_x)
    ]

    lax.fori_loop(tiles // 2, tiles, long_local, 0)

    above = jnp.zeros((POLES, half), F32)
    for step in range(1, n_x):
        x_copies[step - 1].wait_recv()
        above += jnp.where(
            x_pos >= step, jnp.exp(-rates * (row_span * (step - 1))) * rows_seen[step - 1], 0.0
        )
    before += jnp.exp(-rates * (chip_span * y_pos.astype(F32))) * above
    after = block_decay * before + first
    carry_own[...] = jnp.where(core == 0, before, after)
    carry_away[...] = jnp.where(core == 0, after, before)
    carry_copy = send(carry_away, carry_seen, {"seq": other})

    short_conv(query_own, query_halo, 0, query_tilde)
    squares[...] = jnp.zeros_like(squares)

    def gate(group, carry, carry_group):
        cols = lanes(group * LANES, LANES)
        of = lanes(carry_group * LANES, LANES)
        steps = [eighth[pole, :, cols] for pole in range(POLES)]
        start = []
        for pole in range(POLES):
            one = pl.ds(pole, 1)
            weight = residues[one, cols] * carry[one, of] * jnp.exp(-decay_rates[one, cols])
            start.append(weight * powers[pole, :, cols])
        skip = skip_gain[:, cols]

        def rows(number, running):
            top = functools.reduce(jnp.add, running)
            running = [r * s for r, s in zip(running, steps)]
            low = functools.reduce(jnp.add, running)
            running = tuple(r * s for r, s in zip(running, steps))
            at = pl.ds(pl.multiple_of(number * 16, 16), 16)
            long_out = local_long[at, cols] + jnp.concatenate([top, low], 0)
            long_out = long_out.astype(BF).astype(F32)
            total = query_tilde[at, cols].astype(F32) * (
                long_out + skip * mixed[at, cols].astype(F32)
            )
            gated[at, cols] = total
            squares[at, :] += total * total
            return running

        lax.fori_loop(0, ROWS // 16, rows, tuple(start), unroll=2)

    lax.fori_loop(
        0, half_groups, lambda n, _: (gate(core * half_groups + n, carry_own, n), 0)[1], 0
    )
    carry_copy.wait_recv()
    lax.fori_loop(
        0, half_groups, lambda n, _: (gate((1 - core) * half_groups + n, carry_seen, n), 0)[1], 0
    )

    row_sums[...] = jnp.sum(jnp.transpose(squares[...]), axis=0, keepdims=True)
    sum_copies = [
        send(row_sums, sums_seen.at[step - 1], {"chan": (chan + step) % n_z})
        for step in range(1, n_z)
    ]
    total = row_sums[...]
    for step in range(1, n_z):
        sum_copies[step - 1].wait_recv()
        total = total + sums_seen[step - 1]
    scale = lax.rsqrt(total * (1.0 / (channels * n_z)) + 1e-05)
    scale = jnp.transpose(jnp.broadcast_to(scale, (LANES, ROWS)))

    def finish(group, _):
        cols = lanes(group * LANES, LANES)
        result[:, cols] = (gated[:, cols] * scale * norm_gain[:, cols]).astype(BF)
        return 0

    lax.fori_loop(0, channels // LANES, finish, 0)
    store = pltpu.make_async_copy(result, out, store_sem)
    store.start()
    for copy in sent:
        copy.wait_send()
    store.wait()


def solution(mesh):
    n_seq, n_z = mesh.shape["seq"], mesh.shape["chan"]
    n_y = math.isqrt(n_seq // 2)
    n_x = n_seq // 2 // n_y
    tables = make_tables()

    def local(query, key, value, short_taps, medium_taps, residues, decay_rates, skip, gain):
        channels = query.shape[1]
        half = channels // 2
        n_copies = 3 + 1 + (n_y - 1) + (n_x - 1) + 1 + (n_z - 1)
        vmem = pltpu.VMEM
        scratch = [
            vmem((ROWS, channels), BF),
            vmem((TAPS + EDGE, channels), BF),
            vmem((ROWS, channels), BF),
            vmem((EDGE, channels), BF),
            vmem((ROWS, channels), BF),
            vmem((EDGE, channels), BF),
            vmem((EDGE + ROWS, TILE), F32),
            vmem((ROWS, channels), BF),
            vmem((ROWS, channels), BF),
            vmem((2 * HALF_ONE, channels), F32),
            vmem((2 * HALF_ONE, channels), F32),
            vmem((2 * HALF_TWO, channels), F32),
            vmem((ROWS, channels), F32),
            vmem((POLES, 8, channels), F32),
            vmem((POLES, 8, channels), F32),
            vmem((ROWS, channels), BF),
            vmem((POLES, half), F32),
            vmem((POLES, half), F32),
            vmem((POLES, half), F32),
            vmem((POLES, half), F32),
            vmem((n_y - 1, POLES, half), F32),
            vmem((POLES, half), F32),
            vmem((n_x - 1, POLES, half), F32),
            vmem((POLES, half), F32),
            vmem((POLES, half), F32),
            vmem((POLES, half), F32),
            vmem((ROWS, channels), F32),
            vmem((ROWS, channels), F32),
            vmem((ROWS, LANES), F32),
            vmem((1, ROWS), F32),
            vmem((n_z - 1, 1, ROWS), F32),
            vmem((ROWS, channels), BF),
            pltpu.SemaphoreType.DMA((3,)),
            pltpu.SemaphoreType.DMA((n_copies,)),
            pltpu.SemaphoreType.DMA((n_copies,)),
            pltpu.SemaphoreType.DMA,
        ]
        in_vmem = pl.BlockSpec(memory_space=pltpu.VMEM)
        anywhere = pl.BlockSpec(memory_space=pl.ANY)
        call = pl.pallas_call(
            functools.partial(kernel, (n_x, n_y, n_z, channels)),
            out_shape=jax.ShapeDtypeStruct((ROWS, channels), BF),
            in_specs=[anywhere] * 3 + [in_vmem] * 11,
            out_specs=anywhere,
            scratch_shapes=scratch,
            compiler_params=pltpu.CompilerParams(
                collective_id=0, has_side_effects=True, vmem_limit_bytes=48 * 1024 * 1024
            ),
        )
        return call(
            query,
            key,
            value,
            short_taps,
            medium_taps,
            residues,
            decay_rates,
            skip.reshape(1, channels),
            gain.reshape(1, channels),
            *tables,
        )

    in_specs = (
        P("seq", "chan"),
        P("seq", "chan"),
        P("seq", "chan"),
        P(None, None, "chan"),
        P(None, "chan"),
        P(None, "chan"),
        P(None, "chan"),
        P("chan"),
        P("chan"),
    )
    return jax.shard_map(
        local, mesh=mesh, in_specs=in_specs, out_specs=P("seq", "chan"), check_vma=False
    )
```

```python
import functools
import math

import jax
import jax.numpy as jnp
import ml_dtypes
import numpy as np
from jax import lax
from jax.experimental import pallas as pl
from jax.experimental.pallas import tpu as pltpu
from jax.sharding import PartitionSpec as P

D = 8192
ROWS = 256
TAPS = 128
POLES = 16
LANES = 128
TILE = 256
EDGE = 16
HALF_ONE = 192
HALF_TWO = 256
MESH = pl.DeviceIdType.MESH
BF = jnp.bfloat16
F32 = jnp.float32


def split_np(table):
    high = table.astype(np.float32).astype(ml_dtypes.bfloat16)
    low = (table - high.astype(np.float64)).astype(np.float32).astype(ml_dtypes.bfloat16)
    return np.stack([high, low])


def odd_tables(half, positions):
    angle = (2.0 * math.pi / (2 * half)) * (np.arange(half) + 0.5)[:, None] * positions[None, :]
    return np.concatenate([np.cos(angle), -np.sin(angle)], 0)


def make_tables():
    one = odd_tables(HALF_ONE, np.arange(2 * HALF_ONE))
    two = odd_tables(HALF_TWO, np.arange(ROWS))
    turn = np.zeros((HALF_ONE, LANES), np.float32)
    base = (2.0 * math.pi / (2 * HALF_ONE)) * (np.arange(HALF_ONE) + 0.5)
    turn[:, 0] = np.cos(base)
    turn[:, 1] = np.cos(2 * base)
    turn[:, 2] = -np.sin(base)
    turn[:, 3] = -np.sin(2 * base)
    return (
        split_np(one),
        split_np(one[:, TAPS:].T.copy()),
        split_np(two),
        split_np(two.T.copy()),
        turn,
    )


def run(name, task):
    task()


def split(value):
    high = value.astype(BF)
    return high, (value - high.astype(F32)).astype(BF)


def mm(left, right):
    return jnp.dot(left, right, preferred_element_type=F32)


def kernel(
    dims,
    query,
    key,
    value,
    *rest,
):
    sources, out, buffers, scratch = rest[:11], rest[11], rest[12:23], rest[23:]
    body(dims, query, key, value, sources, out, buffers, *scratch)


def body(
    dims,
    query,
    key,
    value,
    sources,
    out,
    buffers,
    key_own,
    key_halo,
    value_own,
    value_halo,
    query_own,
    query_halo,
    staged,
    value_tilde,
    query_tilde,
    tap_spec,
    key_spec,
    kernel_spec,
    long_kernel,
    powers,
    eighth,
    mixed,
    states_own,
    states_away,
    states_seen,
    chip_state,
    chips_seen,
    row_state,
    rows_seen,
    carry_own,
    carry_away,
    carry_seen,
    local_long,
    gated,
    squares,
    row_sums,
    sums_seen,
    load_sems,
    send_sems,
    recv_sems,
):
    n_x, n_y, n_z, channels = dims
    (
        short_taps,
        medium_taps,
        residues,
        decay_rates,
        skip_gain,
        norm_gain,
        fwd_one,
        inv_one,
        fwd_two,
        inv_two,
        turn,
    ) = buffers
    half = channels // 2
    seq = lax.axis_index("seq")
    chan = lax.axis_index("chan")
    core = seq % 2
    y_pos = (seq // 2) % n_y
    x_pos = seq // (2 * n_y)
    n_seq = 2 * n_x * n_y
    right = (seq + 1) % n_seq
    left = (seq + n_seq - 1) % n_seq
    other = seq + 1 - 2 * core

    def along_y(step):
        return (x_pos * n_y + (y_pos + step) % n_y) * 2 + core

    def along_x(step):
        return (((x_pos + step) % n_x) * n_y + y_pos) * 2 + core

    order = (3, 2, 10, 6, 1, 0, 8, 7, 9, 4, 5)
    pairs = [(sources[n], buffers[n]) for n in order[:2]] + [(key, key_own)]
    pairs += [(sources[n], buffers[n]) for n in order[2:]]
    pairs += [(value, value_own), (query, query_own)]
    loads = [
        pltpu.make_async_copy(source, target, load_sems.at[number])
        for number, (source, target) in enumerate(pairs)
    ]
    for load in loads:
        load.start()

    barrier = pltpu.get_barrier_semaphore()
    seq_partners = [right, left, other]
    seq_partners += [along_y(step) for step in range(1, n_y)]
    seq_partners += [along_x(step) for step in range(1, n_x)]
    for partner in seq_partners:
        pl.semaphore_signal(barrier, inc=1, device_id={"seq": partner}, device_id_type=MESH)
    for step in range(1, n_z):
        pl.semaphore_signal(
            barrier, inc=1, device_id={"chan": (chan + step) % n_z}, device_id_type=MESH
        )
    pl.semaphore_wait(barrier, len(seq_partners) + n_z - 1)

    sent = []

    def send(source, target, where):
        number = len(sent)
        copy = pltpu.make_async_remote_copy(
            src_ref=source,
            dst_ref=target,
            send_sem=send_sems.at[number],
            recv_sem=recv_sems.at[number],
            device_id=where,
            device_id_type=MESH,
        )
        copy.start()
        sent.append(copy)
        return copy

    key_copy = send(key.at[pl.ds(ROWS - TAPS - EDGE, TAPS + EDGE), :], key_halo, {"seq": right})
    value_copy = send(value.at[pl.ds(ROWS - EDGE, EDGE), :], value_halo, {"seq": right})
    query_copy = send(query.at[pl.ds(ROWS - EDGE, EDGE), :], query_halo, {"seq": right})

    def lanes(start, size):
        return pl.ds(pl.multiple_of(start, size), size)

    loads[0].wait()
    loads[1].wait()

    sub = lax.broadcasted_iota(jnp.int32, (8, LANES), 0).astype(F32)

    def pole_powers(group, _):
        cols = lanes(group * LANES, LANES)
        start = []
        steps = []
        for pole in range(POLES):
            rate = decay_rates[pl.ds(pole, 1), cols]
            power = jnp.exp(-rate * sub)
            powers[pole, :, cols] = power
            step = jnp.broadcast_to(jnp.exp(-8.0 * rate), (8, LANES))
            eighth[pole, :, cols] = step
            start.append(residues[pl.ds(pole, 1), cols] * power)
            steps.append(step)

        def rows(number, running):
            total = functools.reduce(jnp.add, running)
            long_kernel[pl.ds(pl.multiple_of(number * 8, 8), 8), cols] = total
            return tuple(r * s for r, s in zip(running, steps))

        lax.fori_loop(0, ROWS // 8, rows, tuple(start), unroll=4)
        return 0

    run("powers", lambda: lax.fori_loop(0, channels // LANES, pole_powers, 0))

    for load in loads[2:8]:
        load.wait()

    def before_halo(tile, _):
        cols = lanes(tile * TILE, TILE)
        taps = medium_taps[:, cols]
        spec = mm(fwd_one[0, :, :TAPS], taps) + mm(fwd_one[1, :, :TAPS], taps)
        first = short_taps[1, :, cols].astype(F32)
        s_re = first[0:1] + first[1:2] * turn[:, 0:1] + first[2:3] * turn[:, 1:2]
        s_im = first[1:2] * turn[:, 2:3] + first[2:3] * turn[:, 3:4]
        m_re, m_im = spec[:HALF_ONE], spec[HALF_ONE:]
        scale = 1.0 / HALF_ONE
        tap_spec[:HALF_ONE, cols] = (m_re * s_re - m_im * s_im) * scale
        tap_spec[HALF_ONE:, cols] = (m_re * s_im + m_im * s_re) * scale
        own = key_own[:, cols]
        key_spec[:, cols] = mm(fwd_one[0, :, TAPS:], own) + mm(fwd_one[1, :, TAPS:], own)
        high, low = split(long_kernel[:, cols])
        spec = mm(fwd_two[0], high) + mm(fwd_two[0], low) + mm(fwd_two[1], high)
        kernel_spec[:, cols] = spec * (1.0 / HALF_TWO)
        return 0

    run("before", lambda: lax.fori_loop(0, channels // TILE, before_halo, 0))

    def short_conv(source, halo, taps_row, target):
        def one(tile, _):
            cols = lanes(tile * TILE, TILE)
            staged[0:EDGE, :] = halo[:, cols].astype(F32)
            staged[EDGE:, :] = source[:, cols].astype(F32)
            weights = short_taps[taps_row, :, cols].astype(F32)
            total = (
                weights[0:1] * staged[EDGE:, :]
                + weights[1:2] * staged[EDGE - 1 : EDGE - 1 + ROWS, :]
                + weights[2:3] * staged[EDGE - 2 : EDGE - 2 + ROWS, :]
            )
            target[:, cols] = total.astype(BF)
            return 0

        lax.fori_loop(0, channels // TILE, one, 0)

    for load in loads[8:]:
        load.wait()
    key_copy.wait_recv()
    value_copy.wait_recv()
    query_copy.wait_recv()

    @pl.when(seq == 0)
    def _():
        key_halo[...] = jnp.zeros_like(key_halo)
        value_halo[...] = jnp.zeros_like(value_halo)
        query_halo[...] = jnp.zeros_like(query_halo)

    run("value", lambda: short_conv(value_own, value_halo, 2, value_tilde))

    def medium(tile):
        cols = lanes(tile * TILE, TILE)
        past = key_halo[EDGE:, cols]
        spec = key_spec[:, cols] + mm(fwd_one[0, :, :TAPS], past) + mm(fwd_one[1, :, :TAPS], past)
        x_re, x_im = spec[:HALF_ONE], spec[HALF_ONE:]
        t_re, t_im = tap_spec[:HALF_ONE, cols], tap_spec[HALF_ONE:, cols]
        re_high, re_low = split(x_re * t_re - x_im * t_im)
        im_high, im_low = split(x_re * t_im + x_im * t_re)
        high = jnp.concatenate([re_high, im_high], 0)
        low = jnp.concatenate([re_low, im_low], 0)
        key_hat = mm(inv_one[0], high) + mm(inv_one[0], low) + mm(inv_one[1], high)
        last = short_taps[1, 2:3, cols].astype(F32) * medium_taps[TAPS - EDGE :, cols].astype(F32)[
            EDGE - 1 :
        ]
        ends = (
            key_halo[:EDGE, cols].astype(F32)[EDGE - 1 :]
            + key_own[ROWS - EDGE :, cols].astype(F32)[EDGE - 1 :]
        )
        row = lax.broadcasted_iota(jnp.int32, (ROWS, TILE), 0)
        key_hat = key_hat + jnp.where(row == 0, last * ends, 0.0)
        mixed[:, cols] = (key_hat * value_tilde[:, cols].astype(F32)).astype(BF)

    def end_states(group, target, target_group):
        cols = lanes(group * LANES, LANES)
        steps = [eighth[pole, :, cols] for pole in range(POLES)]

        def rows(number, running):
            block = mixed[pl.ds(pl.multiple_of(number * 16, 16), 16), cols].astype(F32)
            running = [r * s + block[:8] for r, s in zip(running, steps)]
            return tuple(r * s + block[8:] for r, s in zip(running, steps))

        empty = tuple(jnp.zeros((8, LANES), F32) for _ in range(POLES))
        running = lax.fori_loop(0, ROWS // 16, rows, empty, unroll=2)
        to = lanes(target_group * LANES, LANES)
        for pole in range(POLES):
            rate = decay_rates[pl.ds(pole, 1), cols]
            weighted = running[pole] * jnp.exp(-rate * (7.0 - sub))
            target[pl.ds(pole, 1), to] = jnp.sum(weighted, axis=0, keepdims=True)

    half_tiles = half // TILE
    half_groups = half // LANES

    def half_block(side, target):
        def medium_tile(n, _):
            medium(side * half_tiles + n)
            return 0

        def state_group(n, _):
            end_states(side * half_groups + n, target, n)
            return 0

        run("medium", lambda: lax.fori_loop(0, half_tiles, medium_tile, 0))
        run("states", lambda: lax.fori_loop(0, half_groups, state_group, 0))

    half_block(1 - core, states_away)
    states_copy = send(states_away, states_seen, {"seq": other})
    half_block(core, states_own)

    own_cols = lanes(core * half, half)
    rates = decay_rates[:, own_cols]
    block_decay = jnp.exp(-float(ROWS) * rates)
    states_copy.wait_recv()
    mine, theirs = states_own[...], states_seen[...]
    first = jnp.where(core == 0, mine, theirs)
    second = jnp.where(core == 0, theirs, mine)
    chip_state[...] = block_decay * first + second
    y_copies = [
        send(chip_state, chips_seen.at[step - 1], {"seq": along_y(step)}) for step in range(1, n_y)
    ]

    def long_local(tile, _):
        cols = lanes(tile * TILE, TILE)
        signal = mixed[:, cols]
        spec = mm(fwd_two[0], signal) + mm(fwd_two[1], signal)
        x_re, x_im = spec[:HALF_TWO], spec[HALF_TWO:]
        k_re, k_im = kernel_spec[:HALF_TWO, cols], kernel_spec[HALF_TWO:, cols]
        re_high, re_low = split(x_re * k_re - x_im * k_im)
        im_high, im_low = split(x_re * k_im + x_im * k_re)
        high = jnp.concatenate([re_high, im_high], 0)
        low = jnp.concatenate([re_low, im_low], 0)
        local_long[:, cols] = mm(inv_two[0], high) + mm(inv_two[0], low) + mm(inv_two[1], high)
        return 0

    tiles = channels // TILE
    run("long1", lambda: lax.fori_loop(0, tiles // 2, long_local, 0))

    chip_span = float(2 * ROWS)
    row_span = float(2 * ROWS * n_y)
    y_far = (n_y - 1 - y_pos).astype(F32)
    row_total = jnp.exp(-rates * (chip_span * y_far)) * chip_state[...]
    before = jnp.zeros((POLES, half), F32)
    for step in range(1, n_y):
        y_copies[step - 1].wait_recv()
        seen = chips_seen[step - 1]
        source = (y_pos - step + n_y) % n_y
        distance = (n_y - 1 - source).astype(F32)
        row_total += jnp.exp(-rates * (chip_span * distance)) * seen
        before += jnp.where(y_pos >= step, jnp.exp(-rates * (chip_span * (step - 1))) * seen, 0.0)
    row_state[...] = row_total
    x_copies = [
        send(row_state, rows_seen.at[step - 1], {"seq": along_x(step)}) for step in range(1, n_x)
    ]

    run("long2", lambda: lax.fori_loop(tiles // 2, tiles, long_local, 0))

    above = jnp.zeros((POLES, half), F32)
    for step in range(1, n_x):
        x_copies[step - 1].wait_recv()
        above += jnp.where(
            x_pos >= step, jnp.exp(-rates * (row_span * (step - 1))) * rows_seen[step - 1], 0.0
        )
    before += jnp.exp(-rates * (chip_span * y_pos.astype(F32))) * above
    after = block_decay * before + first
    carry_own[...] = jnp.where(core == 0, before, after)
    carry_away[...] = jnp.where(core == 0, after, before)
    carry_copy = send(carry_away, carry_seen, {"seq": other})

    run("query", lambda: short_conv(query_own, query_halo, 0, query_tilde))
    squares[...] = jnp.zeros_like(squares)

    def gate(group, carry, carry_group):
        cols = lanes(group * LANES, LANES)
        of = lanes(carry_group * LANES, LANES)
        steps = [eighth[pole, :, cols] for pole in range(POLES)]
        start = []
        for pole in range(POLES):
            one = pl.ds(pole, 1)
            weight = residues[one, cols] * carry[one, of] * jnp.exp(-decay_rates[one, cols])
            start.append(weight * powers[pole, :, cols])
        skip = skip_gain[:, cols]

        def rows(number, running):
            top = functools.reduce(jnp.add, running)
            running = [r * s for r, s in zip(running, steps)]
            low = functools.reduce(jnp.add, running)
            running = tuple(r * s for r, s in zip(running, steps))
            at = pl.ds(pl.multiple_of(number * 16, 16), 16)
            long_out = local_long[at, cols] + jnp.concatenate([top, low], 0)
            long_out = long_out.astype(BF).astype(F32)
            total = query_tilde[at, cols].astype(F32) * (
                long_out + skip * mixed[at, cols].astype(F32)
            )
            gated[at, cols] = total
            squares[at, :] += total * total
            return running

        lax.fori_loop(0, ROWS // 16, rows, tuple(start), unroll=2)

    def gate_half(side, carry):
        def one(n, _):
            gate(side * half_groups + n, carry, n)
            return 0

        run("gate", lambda: lax.fori_loop(0, half_groups, one, 0))

    gate_half(core, carry_own)
    carry_copy.wait_recv()
    gate_half(1 - core, carry_seen)

    row_sums[...] = jnp.sum(jnp.transpose(squares[...]), axis=0, keepdims=True)
    sum_copies = [
        send(row_sums, sums_seen.at[step - 1], {"chan": (chan + step) % n_z})
        for step in range(1, n_z)
    ]
    total = row_sums[...]
    for step in range(1, n_z):
        sum_copies[step - 1].wait_recv()
        total = total + sums_seen[step - 1]
    scale = lax.rsqrt(total * (1.0 / (channels * n_z)) + 1e-05)
    scale = jnp.transpose(jnp.broadcast_to(scale, (LANES, ROWS)))

    def finish(group, _):
        cols = lanes(group * LANES, LANES)
        out[:, cols] = (gated[:, cols] * scale * norm_gain[:, cols]).astype(BF)
        return 0

    run("finish", lambda: lax.fori_loop(0, channels // LANES, finish, 0))
    for copy in sent:
        copy.wait_send()


def solution(mesh):
    n_seq, n_z = mesh.shape["seq"], mesh.shape["chan"]
    n_y = math.isqrt(n_seq // 2)
    n_x = n_seq // 2 // n_y
    tables = make_tables()

    def local(query, key, value, short_taps, medium_taps, residues, decay_rates, skip, gain):
        channels = query.shape[1]
        half = channels // 2
        operands = (
            query,
            key,
            value,
            short_taps,
            medium_taps,
            residues,
            decay_rates,
            skip.reshape(1, channels),
            gain.reshape(1, channels),
            *(jnp.asarray(table) for table in tables),
        )
        n_copies = 3 + 1 + (n_y - 1) + (n_x - 1) + 1 + (n_z - 1)
        vmem = pltpu.VMEM
        scratch = [
            vmem((ROWS, channels), BF),
            vmem((TAPS + EDGE, channels), BF),
            vmem((ROWS, channels), BF),
            vmem((EDGE, channels), BF),
            vmem((ROWS, channels), BF),
            vmem((EDGE, channels), BF),
            vmem((EDGE + ROWS, TILE), F32),
            vmem((ROWS, channels), BF),
            vmem((ROWS, channels), BF),
            vmem((2 * HALF_ONE, channels), F32),
            vmem((2 * HALF_ONE, channels), F32),
            vmem((2 * HALF_TWO, channels), F32),
            vmem((ROWS, channels), F32),
            vmem((POLES, 8, channels), F32),
            vmem((POLES, 8, channels), F32),
            vmem((ROWS, channels), BF),
            vmem((POLES, half), F32),
            vmem((POLES, half), F32),
            vmem((POLES, half), F32),
            vmem((POLES, half), F32),
            vmem((n_y - 1, POLES, half), F32),
            vmem((POLES, half), F32),
            vmem((n_x - 1, POLES, half), F32),
            vmem((POLES, half), F32),
            vmem((POLES, half), F32),
            vmem((POLES, half), F32),
            vmem((ROWS, channels), F32),
            vmem((ROWS, channels), F32),
            vmem((ROWS, LANES), F32),
            vmem((1, ROWS), F32),
            vmem((n_z - 1, 1, ROWS), F32),
            pltpu.SemaphoreType.DMA((len(operands),)),
            pltpu.SemaphoreType.DMA((n_copies,)),
            pltpu.SemaphoreType.DMA((n_copies,)),
        ]
        in_hbm = pl.BlockSpec(memory_space=pltpu.HBM)
        call = pl.pallas_call(
            functools.partial(kernel, (n_x, n_y, n_z, channels)),
            out_shape=jax.ShapeDtypeStruct((ROWS, channels), BF),
            in_specs=[in_hbm] * len(operands),
            out_specs=pl.BlockSpec(memory_space=pltpu.VMEM),
            scratch_shapes=[vmem(x.shape, x.dtype) for x in operands[3:]] + scratch,
            compiler_params=pltpu.CompilerParams(
                collective_id=0, has_side_effects=True, vmem_limit_bytes=60 * 1024 * 1024
            ),
        )
        return call(*operands)

    in_specs = (
        P("seq", "chan"),
        P("seq", "chan"),
        P("seq", "chan"),
        P(None, None, "chan"),
        P(None, "chan"),
        P(None, "chan"),
        P(None, "chan"),
        P("chan"),
        P("chan"),
    )
    return jax.shard_map(
        local, mesh=mesh, in_specs=in_specs, out_specs=P("seq", "chan"), check_vma=False
    )
```

```python
import functools
import math

import jax
import jax.numpy as jnp
import ml_dtypes
import numpy as np
from jax import lax
from jax.experimental import pallas as pl
from jax.experimental.pallas import tpu as pltpu
from jax.sharding import PartitionSpec as P

D = 8192
ROWS = 256
TAPS = 128
POLES = 16
LANES = 128
TILE = 256
EDGE = 16
HALF_ONE = 192
HALF_TWO = 256
MESH = pl.DeviceIdType.MESH
BF = jnp.bfloat16
F32 = jnp.float32


def narrow(table):
    return np.ascontiguousarray(table).astype(np.float32).astype(ml_dtypes.bfloat16)


def odd_tables(half, positions):
    angle = (2.0 * math.pi / (2 * half)) * (np.arange(half) + 0.5)[:, None] * positions[None, :]
    return np.concatenate([np.cos(angle), -np.sin(angle)], 0)


def make_tables():
    one = odd_tables(HALF_ONE, np.arange(2 * HALF_ONE))
    two = odd_tables(HALF_TWO, np.arange(ROWS))
    turn = np.zeros((HALF_ONE, LANES), np.float32)
    base = (2.0 * math.pi / (2 * HALF_ONE)) * (np.arange(HALF_ONE) + 0.5)
    turn[:, 0] = np.cos(base)
    turn[:, 1] = np.cos(2 * base)
    turn[:, 2] = -np.sin(base)
    turn[:, 3] = -np.sin(2 * base)
    return (
        narrow(one),
        narrow(one[:, TAPS:].T),
        narrow(two),
        narrow(two.T),
        turn,
    )


def run(name, task):
    task()


def split(value):
    high = value.astype(BF)
    return high, (value - high.astype(F32)).astype(BF)


def mm(left, right):
    return jnp.dot(left, right, preferred_element_type=F32)


def kernel(
    dims,
    query,
    key,
    value,
    *rest,
):
    sources, out, buffers, scratch = rest[:11], rest[11], rest[12:23], rest[23:]
    body(dims, query, key, value, sources, out, buffers, *scratch)


def body(
    dims,
    query,
    key,
    value,
    sources,
    out,
    buffers,
    key_own,
    key_halo,
    value_own,
    value_halo,
    query_own,
    query_halo,
    staged,
    value_tilde,
    query_tilde,
    tap_spec,
    key_spec,
    kernel_spec,
    long_kernel,
    powers,
    eighth,
    mixed,
    states_own,
    states_away,
    states_seen,
    chip_state,
    chips_seen,
    row_state,
    rows_seen,
    carry_own,
    carry_away,
    carry_seen,
    local_long,
    gated,
    squares,
    row_sums,
    sums_seen,
    load_sems,
    send_sems,
    recv_sems,
    y_relay,
    x_relay,
    z_relay,
):
    n_x, n_y, n_z, channels = dims
    (
        short_taps,
        medium_taps,
        residues,
        decay_rates,
        skip_gain,
        norm_gain,
        fwd_one,
        inv_one,
        fwd_two,
        inv_two,
        turn,
    ) = buffers
    half = channels // 2
    seq = lax.axis_index("seq")
    chan = lax.axis_index("chan")
    core = seq % 2
    y_pos = (seq // 2) % n_y
    x_pos = seq // (2 * n_y)
    n_seq = 2 * n_x * n_y
    right = (seq + 1) % n_seq
    left = (seq + n_seq - 1) % n_seq
    other = seq + 1 - 2 * core

    def along_y(step):
        return (x_pos * n_y + (y_pos + step) % n_y) * 2 + core

    def along_z(step):
        return {"chan": (chan + step) % n_z}

    def lanes(start, size):
        return pl.ds(pl.multiple_of(start, size), size)

    def along_x(step):
        return (((x_pos + step) % n_x) * n_y + y_pos) * 2 + core

    pairs = [(sources[n], buffers[n]) for n in (3, 6, 1, 0, 10)] + [(key, key_own)]
    pairs += [(value, value_own)] + [(sources[n], buffers[n]) for n in (2, 7, 8, 9, 4, 5)]
    pairs += [(query, query_own)]
    loads = [
        pltpu.make_async_copy(source, target, load_sems.at[number])
        for number, (source, target) in enumerate(pairs)
    ]
    for load in loads:
        load.start()

    barrier = pltpu.get_barrier_semaphore()
    near = [{"seq": right}, {"seq": left}, {"seq": other}]
    near += [{"seq": along_y(1)}, {"seq": along_y(n_y - 1)}]
    near += [{"seq": along_x(1)}, {"seq": along_x(n_x - 1)}]
    near += [along_z(1), along_z(n_z - 1)]
    for partner in near:
        pl.semaphore_signal(barrier, inc=1, device_id=partner, device_id_type=MESH)

    sub = lax.broadcasted_iota(jnp.int32, (8, LANES), 0).astype(F32)
    loads[0].wait()

    def pole_powers(group, _):
        cols = lanes(group * LANES, LANES)
        for pole in range(POLES):
            rate = decay_rates[pl.ds(pole, 1), cols]
            powers[pole, :, cols] = jnp.exp(-rate * sub)
            eighth[pole, :, cols] = jnp.broadcast_to(jnp.exp(-8.0 * rate), (8, LANES))
        return 0

    run("powers", lambda: lax.fori_loop(0, channels // LANES, pole_powers, 0))
    pl.semaphore_wait(barrier, len(near))

    def relay(sems, along, size, step):
        for way, sign in enumerate((1, size - 1)):
            pl.semaphore_signal(
                sems.at[step - 2, way], inc=1, device_id=along(sign), device_id_type=MESH
            )

    def relayed(sems, step):
        for way in range(2):
            pl.semaphore_wait(sems.at[step - 2, way], 1)

    def seq_y(step):
        return {"seq": along_y(step)}

    def seq_x(step):
        return {"seq": along_x(step)}

    for step in range(2, n_y // 2 + 1):
        relay(y_relay, seq_y, n_y, step)
        relayed(y_relay, step) if step < n_y // 2 else None
    for step in range(2, n_x // 2 + 1):
        relay(x_relay, seq_x, n_x, step)
        relayed(x_relay, step) if step < n_x // 2 else None
    if n_z > 3:
        relay(z_relay, along_z, n_z, 2)

    sent = []

    def send(source, target, where):
        number = len(sent)
        copy = pltpu.make_async_remote_copy(
            src_ref=source,
            dst_ref=target,
            send_sem=send_sems.at[number],
            recv_sem=recv_sems.at[number],
            device_id=where,
            device_id_type=MESH,
        )
        copy.start()
        sent.append(copy)
        return copy

    tiles = channels // TILE
    half_tiles = half // TILE
    half_groups = half // LANES

    def chunk(side, number):
        return (side if number < half_tiles else 1 - side) * half_tiles + number % half_tiles

    key_copies = []
    for number in range(tiles):
        piece = key.at[
            pl.ds(ROWS - TAPS - EDGE, TAPS + EDGE), lanes(chunk(core, number) * TILE, TILE)
        ]
        key_copies.append(send(piece, key_halo.at[number], {"seq": right}))
        if number == 0:
            value_copy = send(value.at[pl.ds(ROWS - EDGE, EDGE), :], value_halo, {"seq": right})
    query_copy = send(query.at[pl.ds(ROWS - EDGE, EDGE), :], query_halo, {"seq": right})

    for load in loads[1:6]:
        load.wait()

    def before_halo(tile, _):
        cols = lanes(tile * TILE, TILE)
        taps = medium_taps[:, cols]
        spec = mm(fwd_one[:, :TAPS], taps)
        first = short_taps[1, :, cols].astype(F32)
        s_re = first[0:1] + first[1:2] * turn[:, 0:1] + first[2:3] * turn[:, 1:2]
        s_im = first[1:2] * turn[:, 2:3] + first[2:3] * turn[:, 3:4]
        m_re, m_im = spec[:HALF_ONE], spec[HALF_ONE:]
        scale = 1.0 / HALF_ONE
        tap_spec[:HALF_ONE, cols] = (m_re * s_re - m_im * s_im) * scale
        tap_spec[HALF_ONE:, cols] = (m_re * s_im + m_im * s_re) * scale
        key_spec[:, cols] = mm(fwd_one[:, TAPS:], key_own[:, cols])
        return 0

    run("before", lambda: lax.fori_loop(0, channels // TILE, before_halo, 0))

    def short_conv(source, halo, taps_row, target, count):
        def one(tile, _):
            cols = lanes(tile * TILE, TILE)
            if halo is None:
                staged[0:EDGE, :] = jnp.zeros((EDGE, TILE), F32)
            else:
                staged[0:EDGE, :] = halo[:, cols].astype(F32)
            staged[EDGE : EDGE + count, :] = source[0:count, cols].astype(F32)
            weights = short_taps[taps_row, :, cols].astype(F32)
            total = (
                weights[0:1] * staged[EDGE : EDGE + count, :]
                + weights[1:2] * staged[EDGE - 1 : EDGE - 1 + count, :]
                + weights[2:3] * staged[EDGE - 2 : EDGE - 2 + count, :]
            )
            target[0:count, cols] = total.astype(BF)
            return 0

        lax.fori_loop(0, tiles, one, 0)

    for load in loads[6:8]:
        load.wait()
    run("value", lambda: short_conv(value_own, None, 2, value_tilde, ROWS))

    def pole_kernel(group, _):
        cols = lanes(group * LANES, LANES)
        steps = [eighth[pole, :, cols] for pole in range(POLES)]
        start = [residues[pl.ds(pole, 1), cols] * powers[pole, :, cols] for pole in range(POLES)]

        def rows(number, running):
            total = functools.reduce(jnp.add, running)
            long_kernel[pl.ds(pl.multiple_of(number * 8, 8), 8), cols] = total
            return tuple(r * s for r, s in zip(running, steps))

        lax.fori_loop(0, ROWS // 8, rows, tuple(start), unroll=4)
        return 0

    run("kernel", lambda: lax.fori_loop(0, channels // LANES, pole_kernel, 0))

    for load in loads[8:]:
        load.wait()

    def medium(number, tile):
        cols = lanes(tile * TILE, TILE)
        spec = key_spec[:, cols] + mm(fwd_one[:, :TAPS], key_halo[number, EDGE:])
        x_re, x_im = spec[:HALF_ONE], spec[HALF_ONE:]
        t_re, t_im = tap_spec[:HALF_ONE, cols], tap_spec[HALF_ONE:, cols]
        re, im = x_re * t_re - x_im * t_im, x_re * t_im + x_im * t_re
        key_hat = mm(inv_one[...], jnp.concatenate([re.astype(BF), im.astype(BF)], 0))
        last = short_taps[1, 2:3, cols].astype(F32) * medium_taps[TAPS - EDGE :, cols].astype(F32)[
            EDGE - 1 :
        ]
        ends = (
            key_halo[number, :EDGE].astype(F32)[EDGE - 1 :]
            + key_own[ROWS - EDGE :, cols].astype(F32)[EDGE - 1 :]
        )
        row = lax.broadcasted_iota(jnp.int32, (ROWS, TILE), 0)
        key_hat = key_hat + jnp.where(row == 0, last * ends, 0.0)
        mixed[:, cols] = (key_hat * value_tilde[:, cols].astype(F32)).astype(BF)

    def end_states(group, target, target_group):
        cols = lanes(group * LANES, LANES)
        steps = [eighth[pole, :, cols] for pole in range(POLES)]

        def rows(number, running):
            block = mixed[pl.ds(pl.multiple_of(number * 16, 16), 16), cols].astype(F32)
            running = [r * s + block[:8] for r, s in zip(running, steps)]
            return tuple(r * s + block[8:] for r, s in zip(running, steps))

        empty = tuple(jnp.zeros((8, LANES), F32) for _ in range(POLES))
        running = lax.fori_loop(0, ROWS // 16, rows, empty, unroll=2)
        to = lanes(target_group * LANES, LANES)
        for pole in range(POLES):
            rate = decay_rates[pl.ds(pole, 1), cols]
            weighted = running[pole] * jnp.exp(-rate * (7.0 - sub))
            target[pl.ds(pole, 1), to] = jnp.sum(weighted, axis=0, keepdims=True)

    def medium_chunk(number, target):
        key_copies[number].wait_recv()

        @pl.when(seq == 0)
        def _():
            key_halo[number] = jnp.zeros((TAPS + EDGE, TILE), BF)

        if number == 0:
            value_copy.wait_recv()

            @pl.when(seq == 0)
            def _():
                value_halo[...] = jnp.zeros_like(value_halo)

            short_conv(value_own, value_halo, 2, value_tilde, EDGE)
        tile = chunk(1 - core, number)
        groups = TILE // LANES

        def state_group(n, _):
            end_states(tile * groups + n, target, number % half_tiles * groups + n)
            return 0

        run("medium", lambda: medium(number, tile))
        run("states", lambda: lax.fori_loop(0, groups, state_group, 0))

    for number in range(half_tiles):
        medium_chunk(number, states_away)
    states_copy = send(states_away, states_seen, {"seq": other})
    for number in range(half_tiles, tiles):
        medium_chunk(number, states_own)

    own_cols = lanes(core * half, half)
    rates = decay_rates[:, own_cols]
    block_decay = jnp.exp(-float(ROWS) * rates)
    states_copy.wait_recv()
    mine, theirs = states_own[...], states_seen[...]
    first = jnp.where(core == 0, mine, theirs)
    second = jnp.where(core == 0, theirs, mine)
    chip_total = block_decay * first + second
    chip_state[...] = chip_total.astype(BF)
    if n_y > 3:
        relayed(y_relay, n_y // 2)
    y_copies = [
        send(chip_state, chips_seen.at[step - 1], {"seq": along_y(step)}) for step in range(1, n_y)
    ]

    def long_local(tile, _):
        cols = lanes(tile * TILE, TILE)
        signal = mixed[:, cols]
        spec = mm(fwd_two[...], signal)
        x_re, x_im = spec[:HALF_TWO], spec[HALF_TWO:]
        k_re, k_im = kernel_spec[:HALF_TWO, cols], kernel_spec[HALF_TWO:, cols]
        re, im = x_re * k_re - x_im * k_im, x_re * k_im + x_im * k_re
        local_long[:, cols] = mm(inv_two[...], jnp.concatenate([re.astype(BF), im.astype(BF)], 0))
        return 0

    def kernel_spectrum(tile, _):
        cols = lanes(tile * TILE, TILE)
        high, low = split(long_kernel[:, cols])
        spec = mm(fwd_two[...], high) + mm(fwd_two[...], low)
        kernel_spec[:, cols] = spec * (1.0 / HALF_TWO)
        return 0

    run("kspec", lambda: lax.fori_loop(0, tiles, kernel_spectrum, 0))
    run("long1", lambda: lax.fori_loop(0, tiles // 2, long_local, 0))
    if n_z > 3:
        relayed(z_relay, 2)
    if n_z > 5:
        relay(z_relay, along_z, n_z, 3)

    chip_span = float(2 * ROWS)
    row_span = float(2 * ROWS * n_y)
    y_far = (n_y - 1 - y_pos).astype(F32)
    row_total = jnp.exp(-rates * (chip_span * y_far)) * chip_total
    before = jnp.zeros((POLES, half), F32)
    for step in range(1, n_y):
        y_copies[step - 1].wait_recv()
        seen = chips_seen[step - 1].astype(F32)
        source = (y_pos - step + n_y) % n_y
        distance = (n_y - 1 - source).astype(F32)
        row_total += jnp.exp(-rates * (chip_span * distance)) * seen
        before += jnp.where(y_pos >= step, jnp.exp(-rates * (chip_span * (step - 1))) * seen, 0.0)
    row_state[...] = row_total.astype(BF)
    if n_x > 3:
        relayed(x_relay, n_x // 2)
    x_copies = [
        send(row_state, rows_seen.at[step - 1], {"seq": along_x(step)}) for step in range(1, n_x)
    ]

    run("long2", lambda: lax.fori_loop(tiles // 2, tiles, long_local, 0))
    query_copy.wait_recv()

    @pl.when(seq == 0)
    def _():
        query_halo[...] = jnp.zeros_like(query_halo)

    run("query", lambda: short_conv(query_own, query_halo, 0, query_tilde, ROWS))
    squares[...] = jnp.zeros_like(squares)
    for step in range(3, n_z // 2 + 1):
        relayed(z_relay, step)
        if step < n_z // 2:
            relay(z_relay, along_z, n_z, step + 1)

    above = jnp.zeros((POLES, half), F32)
    for step in range(1, n_x):
        x_copies[step - 1].wait_recv()
        above += jnp.where(
            x_pos >= step,
            jnp.exp(-rates * (row_span * (step - 1))) * rows_seen[step - 1].astype(F32),
            0.0,
        )
    before += jnp.exp(-rates * (chip_span * y_pos.astype(F32))) * above
    after = block_decay * before + first
    carry_own[...] = jnp.where(core == 0, before, after)
    carry_away[...] = jnp.where(core == 0, after, before)
    carry_copy = send(carry_away, carry_seen, {"seq": other})


    def gate(group, carry, carry_group):
        cols = lanes(group * LANES, LANES)
        of = lanes(carry_group * LANES, LANES)
        steps = [eighth[pole, :, cols] for pole in range(POLES)]
        start = []
        for pole in range(POLES):
            one = pl.ds(pole, 1)
            weight = residues[one, cols] * carry[one, of] * jnp.exp(-decay_rates[one, cols])
            start.append(weight * powers[pole, :, cols])
        skip = skip_gain[:, cols]

        def rows(number, running):
            top = functools.reduce(jnp.add, running)
            running = [r * s for r, s in zip(running, steps)]
            low = functools.reduce(jnp.add, running)
            running = tuple(r * s for r, s in zip(running, steps))
            at = pl.ds(pl.multiple_of(number * 16, 16), 16)
            long_out = local_long[at, cols] + jnp.concatenate([top, low], 0)
            long_out = long_out.astype(BF).astype(F32)
            total = query_tilde[at, cols].astype(F32) * (
                long_out + skip * mixed[at, cols].astype(F32)
            )
            gated[at, cols] = total
            squares[at, :] += total * total
            return running

        lax.fori_loop(0, ROWS // 16, rows, tuple(start), unroll=4)

    def gate_half(side, carry):
        def one(n, _):
            gate(side * half_groups + n, carry, n)
            return 0

        run("gate", lambda: lax.fori_loop(0, half_groups, one, 0))

    gate_half(core, carry_own)
    carry_copy.wait_recv()
    gate_half(1 - core, carry_seen)

    row_sums[...] = jnp.sum(jnp.transpose(squares[...]), axis=0, keepdims=True)
    sum_copies = [
        send(row_sums, sums_seen.at[step - 1], along_z(step)) for step in range(1, n_z)
    ]
    total = row_sums[...]
    for step in range(1, n_z):
        sum_copies[step - 1].wait_recv()
        total = total + sums_seen[step - 1]
    scale = lax.rsqrt(total * (1.0 / (channels * n_z)) + 1e-05)
    scale = jnp.transpose(jnp.broadcast_to(scale, (LANES, ROWS)))

    def finish(group, _):
        cols = lanes(group * LANES, LANES)
        out[:, cols] = gated[:, cols] * scale * norm_gain[:, cols]
        return 0

    run("finish", lambda: lax.fori_loop(0, channels // LANES, finish, 0))
    for copy in sent:
        copy.wait_send()


def solution(mesh):
    n_seq, n_z = mesh.shape["seq"], mesh.shape["chan"]
    n_y = math.isqrt(n_seq // 2)
    n_x = n_seq // 2 // n_y
    tables = make_tables()

    def local(query, key, value, short_taps, medium_taps, residues, decay_rates, skip, gain):
        channels = query.shape[1]
        half = channels // 2
        operands = (
            query,
            key,
            value,
            short_taps,
            medium_taps,
            residues,
            decay_rates,
            skip.reshape(1, channels),
            gain.reshape(1, channels),
            *(jnp.asarray(table) for table in tables),
        )
        tiles = channels // TILE
        n_copies = tiles + 2 + 1 + (n_y - 1) + (n_x - 1) + 1 + (n_z - 1)
        vmem = pltpu.VMEM
        scratch = [
            vmem((ROWS, channels), BF),
            vmem((tiles, TAPS + EDGE, TILE), BF),
            vmem((ROWS, channels), BF),
            vmem((EDGE, channels), BF),
            vmem((ROWS, channels), BF),
            vmem((EDGE, channels), BF),
            vmem((EDGE + ROWS, TILE), F32),
            vmem((ROWS, channels), BF),
            vmem((ROWS, channels), BF),
            vmem((2 * HALF_ONE, channels), F32),
            vmem((2 * HALF_ONE, channels), F32),
            vmem((2 * HALF_TWO, channels), F32),
            vmem((ROWS, channels), F32),
            vmem((POLES, 8, channels), F32),
            vmem((POLES, 8, channels), F32),
            vmem((ROWS, channels), BF),
            vmem((POLES, half), F32),
            vmem((POLES, half), F32),
            vmem((POLES, half), F32),
            vmem((POLES, half), BF),
            vmem((n_y - 1, POLES, half), BF),
            vmem((POLES, half), BF),
            vmem((n_x - 1, POLES, half), BF),
            vmem((POLES, half), F32),
            vmem((POLES, half), F32),
            vmem((POLES, half), F32),
            vmem((ROWS, channels), F32),
            vmem((ROWS, channels), F32),
            vmem((ROWS, LANES), F32),
            vmem((1, ROWS), F32),
            vmem((n_z - 1, 1, ROWS), F32),
            pltpu.SemaphoreType.DMA((len(operands),)),
            pltpu.SemaphoreType.DMA((n_copies,)),
            pltpu.SemaphoreType.DMA((n_copies,)),
            *(
                pltpu.SemaphoreType.REGULAR((max(1, size // 2 - 1), 2))
                for size in (n_y, n_x, n_z)
            ),
        ]
        in_hbm = pl.BlockSpec(memory_space=pltpu.HBM)
        call = pl.pallas_call(
            functools.partial(kernel, (n_x, n_y, n_z, channels)),
            out_shape=jax.ShapeDtypeStruct((ROWS, channels), F32),
            in_specs=[in_hbm] * len(operands),
            out_specs=pl.BlockSpec(memory_space=pltpu.VMEM),
            scratch_shapes=[vmem(x.shape, x.dtype) for x in operands[3:]] + scratch,
            compiler_params=pltpu.CompilerParams(
                collective_id=0, has_side_effects=True, vmem_limit_bytes=60 * 1024 * 1024
            ),
        )
        return call(*operands).astype(BF)

    in_specs = (
        P("seq", "chan"),
        P("seq", "chan"),
        P("seq", "chan"),
        P(None, None, "chan"),
        P(None, "chan"),
        P(None, "chan"),
        P(None, "chan"),
        P("chan"),
        P("chan"),
    )
    return jax.shard_map(
        local, mesh=mesh, in_specs=in_specs, out_specs=P("seq", "chan"), check_vma=False
    )
```

```python
import functools
import math

import jax
import jax.numpy as jnp
import ml_dtypes
import numpy as np
from jax import lax
from jax.experimental import pallas as pl
from jax.experimental.pallas import tpu as pltpu
from jax.sharding import PartitionSpec as P

D = 8192
ROWS = 256
TAPS = 128
POLES = 16
LANES = 128
TILE = 256
EDGE = 16
HALF_ONE = 192
HALF_TWO = 256
MESH = pl.DeviceIdType.MESH
BF = jnp.bfloat16
F32 = jnp.float32


def narrow(table):
    return np.ascontiguousarray(table).astype(np.float32).astype(ml_dtypes.bfloat16)


def odd_tables(half, positions):
    angle = (2.0 * math.pi / (2 * half)) * (np.arange(half) + 0.5)[:, None] * positions[None, :]
    return np.concatenate([np.cos(angle), -np.sin(angle)], 0)


def make_tables():
    one = odd_tables(HALF_ONE, np.arange(2 * HALF_ONE))
    two = odd_tables(HALF_TWO, np.arange(ROWS))
    turn = np.zeros((HALF_ONE, LANES), np.float32)
    base = (2.0 * math.pi / (2 * HALF_ONE)) * (np.arange(HALF_ONE) + 0.5)
    turn[:, 0] = np.cos(base)
    turn[:, 1] = np.cos(2 * base)
    turn[:, 2] = -np.sin(base)
    turn[:, 3] = -np.sin(2 * base)
    return (
        narrow(one),
        narrow(one[:, TAPS:].T),
        narrow(two),
        narrow(two.T),
        turn,
    )


def run(name, task):
    task()


def distance(offset, n_x, n_y):
    down, across = divmod(offset, n_y)
    return min(down, n_x - down) + min(across, n_y - across)


def split(value):
    high = value.astype(BF)
    return high, (value - high.astype(F32)).astype(BF)


def mm(left, right):
    return jnp.dot(left, right, preferred_element_type=F32)


def kernel(
    dims,
    query,
    key,
    value,
    *rest,
):
    sources, out, buffers, scratch = rest[:11], rest[11], rest[12:23], rest[23:]
    body(dims, query, key, value, sources, out, buffers, *scratch)


def body(
    dims,
    query,
    key,
    value,
    sources,
    out,
    buffers,
    key_own,
    key_halo,
    value_own,
    value_halo,
    query_own,
    query_halo,
    staged,
    value_tilde,
    query_tilde,
    tap_spec,
    key_spec,
    kernel_spec,
    long_kernel,
    powers,
    eighth,
    mixed,
    states_own,
    states_away,
    states_seen,
    chip_state,
    chips_seen,
    before_ref,
    carry_own,
    carry_away,
    carry_seen,
    local_long,
    gated,
    query_wide,
    squares,
    row_sums,
    sums_seen,
    load_sems,
    send_sems,
    recv_sems,
    y_relay,
    x_relay,
    z_relay,
    plane_sems,
    chip_send,
    chip_recv,
):
    n_x, n_y, n_z, channels = dims
    (
        short_taps,
        medium_taps,
        residues,
        decay_rates,
        skip_gain,
        norm_gain,
        fwd_one,
        inv_one,
        fwd_two,
        inv_two,
        turn,
    ) = buffers
    half = channels // 2
    seq = lax.axis_index("seq")
    chan = lax.axis_index("chan")
    core = seq % 2
    y_pos = (seq // 2) % n_y
    x_pos = seq // (2 * n_y)
    n_seq = 2 * n_x * n_y
    right = (seq + 1) % n_seq
    left = (seq + n_seq - 1) % n_seq
    other = seq + 1 - 2 * core

    def along_y(step):
        return (x_pos * n_y + (y_pos + step) % n_y) * 2 + core

    def along_z(step):
        return {"chan": (chan + step) % n_z}

    def lanes(start, size):
        return pl.ds(pl.multiple_of(start, size), size)

    def along_x(step):
        return (((x_pos + step) % n_x) * n_y + y_pos) * 2 + core

    pairs = [(sources[n], buffers[n]) for n in (3, 6, 1, 0, 10)] + [(key, key_own)]
    pairs += [(value, value_own)] + [(sources[n], buffers[n]) for n in (2, 7, 8, 9, 4, 5)]
    pairs += [(query, query_own)]
    loads = [
        pltpu.make_async_copy(source, target, load_sems.at[number])
        for number, (source, target) in enumerate(pairs)
    ]
    for load in loads:
        load.start()

    barrier = pltpu.get_barrier_semaphore()
    near = [{"seq": right}, {"seq": left}, {"seq": other}]
    near += [{"seq": along_y(1)}, {"seq": along_y(n_y - 1)}]
    near += [{"seq": along_x(1)}, {"seq": along_x(n_x - 1)}]
    near += [along_z(1), along_z(n_z - 1)]
    for partner in near:
        pl.semaphore_signal(barrier, inc=1, device_id=partner, device_id_type=MESH)

    sub = lax.broadcasted_iota(jnp.int32, (8, LANES), 0).astype(F32)
    loads[0].wait()

    def pole_powers(group, _):
        cols = lanes(group * LANES, LANES)
        for pole in range(POLES):
            rate = decay_rates[pl.ds(pole, 1), cols]
            powers[pole, :, cols] = jnp.exp(-rate * sub)
            eighth[pole, :, cols] = jnp.broadcast_to(jnp.exp(-8.0 * rate), (8, LANES))
        return 0

    run("powers", lambda: lax.fori_loop(0, channels // LANES, pole_powers, 0))
    pl.semaphore_wait(barrier, len(near))

    def relay(sems, along, size, step):
        for way, sign in enumerate((1, size - 1)):
            pl.semaphore_signal(
                sems.at[step - 2, way], inc=1, device_id=along(sign), device_id_type=MESH
            )

    def relayed(sems, step):
        for way in range(2):
            pl.semaphore_wait(sems.at[step - 2, way], 1)

    def seq_y(step):
        return {"seq": along_y(step)}

    def seq_x(step):
        return {"seq": along_x(step)}

    def chip(position):
        return {"seq": position * 2 + core}

    if n_y > 3:
        relay(y_relay, seq_y, n_y, 2)
    if n_x > 3:
        relay(x_relay, seq_x, n_x, 2)
    if n_z > 3:
        relay(z_relay, along_z, n_z, 2)

    sent = []

    def send(source, target, where):
        number = len(sent)
        copy = pltpu.make_async_remote_copy(
            src_ref=source,
            dst_ref=target,
            send_sem=send_sems.at[number],
            recv_sem=recv_sems.at[number],
            device_id=where,
            device_id_type=MESH,
        )
        copy.start()
        sent.append(copy)
        return copy

    tiles = channels // TILE
    half_tiles = half // TILE
    half_groups = half // LANES

    def chunk(side, number):
        return (side if number < half_tiles else 1 - side) * half_tiles + number % half_tiles

    key_copies = []
    for number in range(tiles):
        piece = key.at[
            pl.ds(ROWS - TAPS - EDGE, TAPS + EDGE), lanes(chunk(core, number) * TILE, TILE)
        ]
        key_copies.append(send(piece, key_halo.at[number], {"seq": right}))
        if number == 0:
            value_copy = send(value.at[pl.ds(ROWS - EDGE, EDGE), :], value_halo, {"seq": right})
    query_copy = send(query.at[pl.ds(ROWS - EDGE, EDGE), :], query_halo, {"seq": right})

    for load in loads[1:6]:
        load.wait()

    def before_halo(tile, _):
        cols = lanes(tile * TILE, TILE)
        taps = medium_taps[:, cols]
        spec = mm(fwd_one[:, :TAPS], taps)
        first = short_taps[1, :, cols].astype(F32)
        s_re = first[0:1] + first[1:2] * turn[:, 0:1] + first[2:3] * turn[:, 1:2]
        s_im = first[1:2] * turn[:, 2:3] + first[2:3] * turn[:, 3:4]
        m_re, m_im = spec[:HALF_ONE], spec[HALF_ONE:]
        scale = 1.0 / HALF_ONE
        tap_spec[:HALF_ONE, cols] = (m_re * s_re - m_im * s_im) * scale
        tap_spec[HALF_ONE:, cols] = (m_re * s_im + m_im * s_re) * scale
        key_spec[:, cols] = mm(fwd_one[:, TAPS:], key_own[:, cols])
        return 0

    run("before", lambda: lax.fori_loop(0, channels // TILE, before_halo, 0))

    def short_conv(source, halo, taps_row, target, count):
        def one(tile, _):
            cols = lanes(tile * TILE, TILE)
            if halo is None:
                staged[0:EDGE, :] = jnp.zeros((EDGE, TILE), F32)
            else:
                staged[0:EDGE, :] = halo[:, cols].astype(F32)
            staged[EDGE : EDGE + count, :] = source[0:count, cols].astype(F32)
            weights = short_taps[taps_row, :, cols].astype(F32)
            total = (
                weights[0:1] * staged[EDGE : EDGE + count, :]
                + weights[1:2] * staged[EDGE - 1 : EDGE - 1 + count, :]
                + weights[2:3] * staged[EDGE - 2 : EDGE - 2 + count, :]
            )
            target[0:count, cols] = total.astype(BF)
            return 0

        lax.fori_loop(0, tiles, one, 0)

    for load in loads[6:8]:
        load.wait()
    run("value", lambda: short_conv(value_own, None, 2, value_tilde, ROWS))

    if n_y > 3:
        relayed(y_relay, 2)
    if n_x > 3:
        relayed(x_relay, 2)
    for step in range(1, n_x):
        pl.semaphore_signal(
            plane_sems.at[step - 1], inc=1, device_id=seq_x(step), device_id_type=MESH
        )

    def pole_kernel(group, _):
        cols = lanes(group * LANES, LANES)
        steps = [eighth[pole, :, cols] for pole in range(POLES)]
        start = [residues[pl.ds(pole, 1), cols] * powers[pole, :, cols] for pole in range(POLES)]

        def rows(number, running):
            total = functools.reduce(jnp.add, running)
            long_kernel[pl.ds(pl.multiple_of(number * 8, 8), 8), cols] = total
            return tuple(r * s for r, s in zip(running, steps))

        lax.fori_loop(0, ROWS // 8, rows, tuple(start), unroll=4)
        return 0

    run("kernel", lambda: lax.fori_loop(0, channels // LANES, pole_kernel, 0))

    for load in loads[8:]:
        load.wait()
    if n_z > 5:
        relayed(z_relay, 2)
        relay(z_relay, along_z, n_z, 3)

    def medium(number, tile):
        cols = lanes(tile * TILE, TILE)
        spec = key_spec[:, cols] + mm(fwd_one[:, :TAPS], key_halo[number, EDGE:])
        x_re, x_im = spec[:HALF_ONE], spec[HALF_ONE:]
        t_re, t_im = tap_spec[:HALF_ONE, cols], tap_spec[HALF_ONE:, cols]
        re, im = x_re * t_re - x_im * t_im, x_re * t_im + x_im * t_re
        key_hat = mm(inv_one[...], jnp.concatenate([re.astype(BF), im.astype(BF)], 0))
        last = short_taps[1, 2:3, cols].astype(F32) * medium_taps[TAPS - EDGE :, cols].astype(F32)[
            EDGE - 1 :
        ]
        ends = (
            key_halo[number, :EDGE].astype(F32)[EDGE - 1 :]
            + key_own[ROWS - EDGE :, cols].astype(F32)[EDGE - 1 :]
        )
        row = lax.broadcasted_iota(jnp.int32, (ROWS, TILE), 0)
        key_hat = key_hat + jnp.where(row == 0, last * ends, 0.0)
        mixed[:, cols] = (key_hat * value_tilde[:, cols].astype(F32)).astype(BF)

    def end_states(group, target, target_group):
        cols = lanes(group * LANES, LANES)
        steps = [eighth[pole, :, cols] for pole in range(POLES)]

        def rows(number, running):
            block = mixed[pl.ds(pl.multiple_of(number * 16, 16), 16), cols].astype(F32)
            running = [r * s + block[:8] for r, s in zip(running, steps)]
            return tuple(r * s + block[8:] for r, s in zip(running, steps))

        empty = tuple(jnp.zeros((8, LANES), F32) for _ in range(POLES))
        running = lax.fori_loop(0, ROWS // 16, rows, empty, unroll=2)
        to = lanes(target_group * LANES, LANES)
        for pole in range(POLES):
            rate = decay_rates[pl.ds(pole, 1), cols]
            weighted = running[pole] * jnp.exp(-rate * (7.0 - sub))
            target[pl.ds(pole, 1), to] = jnp.sum(weighted, axis=0, keepdims=True)

    def medium_chunk(number, target):
        key_copies[number].wait_recv()

        @pl.when(seq == 0)
        def _():
            key_halo[number] = jnp.zeros((TAPS + EDGE, TILE), BF)

        if number == 0:
            value_copy.wait_recv()

            @pl.when(seq == 0)
            def _():
                value_halo[...] = jnp.zeros_like(value_halo)

            short_conv(value_own, value_halo, 2, value_tilde, EDGE)
        tile = chunk(1 - core, number)
        groups = TILE // LANES

        def state_group(n, _):
            end_states(tile * groups + n, target, number % half_tiles * groups + n)
            return 0

        run("medium", lambda: medium(number, tile))
        run("states", lambda: lax.fori_loop(0, groups, state_group, 0))

    for number in range(half_tiles):
        medium_chunk(number, states_away)
    states_copy = send(states_away, states_seen, {"seq": other})
    for number in range(half_tiles, tiles):
        medium_chunk(number, states_own)

    for step in range(3, n_z // 2):
        relayed(z_relay, step)
        relay(z_relay, along_z, n_z, step + 1)

    own_cols = lanes(core * half, half)
    rates = decay_rates[:, own_cols]
    block_decay = jnp.exp(-float(ROWS) * rates)
    states_copy.wait_recv()
    mine, theirs = states_own[...], states_seen[...]
    first = jnp.where(core == 0, mine, theirs)
    second = jnp.where(core == 0, theirs, mine)
    chip_state[...] = (block_decay * first + second).astype(BF)
    for step in range(1, n_x):
        pl.semaphore_wait(plane_sems.at[step - 1], 1)
    n_chips = n_x * n_y
    position = seq // 2
    offsets = sorted(range(1, n_chips), key=lambda n: -distance(n, n_x, n_y))
    chip_copies = []
    for offset in offsets:
        copy = pltpu.make_async_remote_copy(
            src_ref=chip_state,
            dst_ref=chips_seen.at[position],
            send_sem=chip_send.at[offset],
            recv_sem=chip_recv.at[position],
            device_id=chip(lax.rem(position + offset, n_chips)),
            device_id_type=MESH,
        )
        pl.when(position + offset < n_chips)(copy.start)
        chip_copies.append((offset, copy))

    def long_local(tile, _):
        cols = lanes(tile * TILE, TILE)
        signal = mixed[:, cols]
        spec = mm(fwd_two[...], signal)
        x_re, x_im = spec[:HALF_TWO], spec[HALF_TWO:]
        k_re, k_im = kernel_spec[:HALF_TWO, cols], kernel_spec[HALF_TWO:, cols]
        re, im = x_re * k_re - x_im * k_im, x_re * k_im + x_im * k_re
        local_long[:, cols] = mm(inv_two[...], jnp.concatenate([re.astype(BF), im.astype(BF)], 0))
        return 0

    def kernel_spectrum(tile, _):
        cols = lanes(tile * TILE, TILE)
        high, low = split(long_kernel[:, cols])
        spec = mm(fwd_two[...], high) + mm(fwd_two[...], low)
        kernel_spec[:, cols] = spec * (1.0 / HALF_TWO)
        return 0

    def pregate(group, _):
        cols = lanes(group * LANES, LANES)
        long_part = local_long[:, cols] + skip_gain[:, cols] * mixed[:, cols].astype(F32)
        wide = query_tilde[:, cols].astype(F32)
        query_wide[:, cols] = wide
        gated[:, cols] = wide * long_part
        return 0

    run("kspec", lambda: lax.fori_loop(0, tiles, kernel_spectrum, 0))
    run("long1", lambda: lax.fori_loop(0, tiles // 2, long_local, 0))

    run("long2", lambda: lax.fori_loop(tiles // 2, tiles, long_local, 0))
    query_copy.wait_recv()

    @pl.when(seq == 0)
    def _():
        query_halo[...] = jnp.zeros_like(query_halo)

    run("query", lambda: short_conv(query_own, query_halo, 0, query_tilde, ROWS))
    run("pregate", lambda: lax.fori_loop(0, channels // LANES, pregate, 0))
    squares[...] = jnp.zeros_like(squares)

    chip_decay = jnp.exp(-float(2 * ROWS) * rates)
    before_ref[...] = jnp.zeros_like(before_ref)
    for source in range(n_chips - 1):

        @pl.when(source < position)
        def _():
            pltpu.make_async_remote_copy(
                src_ref=chip_state,
                dst_ref=chips_seen.at[source],
                send_sem=chip_send.at[0],
                recv_sem=chip_recv.at[source],
                device_id=chip(position),
                device_id_type=MESH,
            ).wait_recv()
            before_ref[...] = before_ref[...] * chip_decay + chips_seen[source].astype(F32)

    before = before_ref[...]
    after = block_decay * before + first
    carry_own[...] = jnp.where(core == 0, before, after)
    carry_away[...] = jnp.where(core == 0, after, before)
    carry_copy = send(carry_away, carry_seen, {"seq": other})


    def gate(group, carry, carry_group):
        cols = lanes(group * LANES, LANES)
        of = lanes(carry_group * LANES, LANES)
        steps = [eighth[pole, :, cols] for pole in range(POLES)]
        start = []
        for pole in range(POLES):
            one = pl.ds(pole, 1)
            weight = residues[one, cols] * carry[one, of] * jnp.exp(-decay_rates[one, cols])
            start.append(weight * powers[pole, :, cols])

        def rows(number, running):
            top = functools.reduce(jnp.add, running)
            running = [r * s for r, s in zip(running, steps)]
            low = functools.reduce(jnp.add, running)
            running = tuple(r * s for r, s in zip(running, steps))
            at = pl.ds(pl.multiple_of(number * 16, 16), 16)
            total = gated[at, cols] + query_wide[at, cols] * jnp.concatenate([top, low], 0)
            gated[at, cols] = total
            squares[at, :] += total * total
            return running

        lax.fori_loop(0, ROWS // 16, rows, tuple(start), unroll=4)

    def gate_half(side, carry):
        def one(n, _):
            gate(side * half_groups + n, carry, n)
            return 0

        run("gate", lambda: lax.fori_loop(0, half_groups, one, 0))

    gate_half(core, carry_own)
    carry_copy.wait_recv()
    gate_half(1 - core, carry_seen)

    row_sums[...] = jnp.sum(jnp.transpose(squares[...]), axis=0, keepdims=True)
    if n_z > 3:
        relayed(z_relay, n_z // 2)
    sum_copies = [
        send(row_sums, sums_seen.at[step - 1], along_z(step)) for step in range(1, n_z)
    ]
    total = row_sums[...]
    for step in range(1, n_z):
        sum_copies[step - 1].wait_recv()
        total = total + sums_seen[step - 1]
    scale = lax.rsqrt(total * (1.0 / (channels * n_z)) + 1e-05)
    scale = jnp.transpose(jnp.broadcast_to(scale, (LANES, ROWS)))

    def finish(group, _):
        cols = lanes(group * LANES, LANES)
        out[:, cols] = (gated[:, cols] * scale * norm_gain[:, cols]).astype(BF)
        return 0

    run("finish", lambda: lax.fori_loop(0, channels // LANES, finish, 0))
    for copy in sent:
        copy.wait_send()
    for offset, copy in chip_copies:
        pl.when(position + offset < n_chips)(copy.wait_send)


def solution(mesh):
    n_seq, n_z = mesh.shape["seq"], mesh.shape["chan"]
    n_y = math.isqrt(n_seq // 2)
    n_x = n_seq // 2 // n_y
    tables = make_tables()

    def local(query, key, value, short_taps, medium_taps, residues, decay_rates, skip, gain):
        channels = query.shape[1]
        half = channels // 2
        operands = (
            query,
            key,
            value,
            short_taps,
            medium_taps,
            residues,
            decay_rates,
            skip.reshape(1, channels),
            gain.reshape(1, channels),
            *(jnp.asarray(table) for table in tables),
        )
        tiles = channels // TILE
        n_copies = tiles + 2 + 1 + 1 + (n_z - 1)
        vmem = pltpu.VMEM
        scratch = [
            vmem((ROWS, channels), BF),
            vmem((tiles, TAPS + EDGE, TILE), BF),
            vmem((ROWS, channels), BF),
            vmem((EDGE, channels), BF),
            vmem((ROWS, channels), BF),
            vmem((EDGE, channels), BF),
            vmem((EDGE + ROWS, TILE), F32),
            vmem((ROWS, channels), BF),
            vmem((ROWS, channels), BF),
            vmem((2 * HALF_ONE, channels), F32),
            vmem((2 * HALF_ONE, channels), F32),
            vmem((2 * HALF_TWO, channels), F32),
            vmem((ROWS, channels), F32),
            vmem((POLES, 8, channels), F32),
            vmem((POLES, 8, channels), F32),
            vmem((ROWS, channels), BF),
            vmem((POLES, half), F32),
            vmem((POLES, half), F32),
            vmem((POLES, half), F32),
            vmem((POLES, half), BF),
            vmem((n_x * n_y, POLES, half), BF),
            vmem((POLES, half), F32),
            vmem((POLES, half), F32),
            vmem((POLES, half), F32),
            vmem((POLES, half), F32),
            vmem((ROWS, channels), F32),
            vmem((ROWS, channels), F32),
            vmem((ROWS, channels), F32),
            vmem((ROWS, LANES), F32),
            vmem((1, ROWS), F32),
            vmem((n_z - 1, 1, ROWS), F32),
            pltpu.SemaphoreType.DMA((len(operands),)),
            pltpu.SemaphoreType.DMA((n_copies,)),
            pltpu.SemaphoreType.DMA((n_copies,)),
            *(
                pltpu.SemaphoreType.REGULAR((max(1, size // 2 - 1), 2))
                for size in (n_y, n_x, n_z)
            ),
            pltpu.SemaphoreType.REGULAR((n_x,)),
            pltpu.SemaphoreType.DMA((n_x * n_y,)),
            pltpu.SemaphoreType.DMA((n_x * n_y,)),
        ]
        in_hbm = pl.BlockSpec(memory_space=pltpu.HBM)
        call = pl.pallas_call(
            functools.partial(kernel, (n_x, n_y, n_z, channels)),
            out_shape=pltpu.VMEM((ROWS, channels), BF),
            in_specs=[in_hbm] * len(operands),
            out_specs=pl.BlockSpec(memory_space=pltpu.VMEM),
            scratch_shapes=[vmem(x.shape, x.dtype) for x in operands[3:]] + scratch,
            compiler_params=pltpu.CompilerParams(
                collective_id=0, has_side_effects=True, vmem_limit_bytes=60 * 1024 * 1024
            ),
        )
        return call(*(pltpu.with_memory_space_constraint(x, pltpu.HBM) for x in operands))

    in_specs = (
        P("seq", "chan"),
        P("seq", "chan"),
        P("seq", "chan"),
        P(None, None, "chan"),
        P(None, "chan"),
        P(None, "chan"),
        P(None, "chan"),
        P("chan"),
        P("chan"),
    )
    return jax.shard_map(
        local, mesh=mesh, in_specs=in_specs, out_specs=P("seq", "chan"), check_vma=False
    )
```

```python
import functools
import math

import jax
import jax.numpy as jnp
import ml_dtypes
import numpy as np
from jax import lax
from jax.experimental import pallas as pl
from jax.experimental.pallas import tpu as pltpu
from jax.sharding import PartitionSpec as P

D = 8192
ROWS = 256
TAPS = 128
POLES = 16
LANES = 128
TILE = 256
EDGE = 16
HALF_ONE = 192
HALF_TWO = 256
MESH = pl.DeviceIdType.MESH
BF = jnp.bfloat16
F32 = jnp.float32


def narrow(table):
    return np.ascontiguousarray(table).astype(np.float32).astype(ml_dtypes.bfloat16)


def odd_tables(half, positions):
    angle = (2.0 * math.pi / (2 * half)) * (np.arange(half) + 0.5)[:, None] * positions[None, :]
    return np.concatenate([np.cos(angle), -np.sin(angle)], 0)


def make_tables():
    one = odd_tables(HALF_ONE, np.arange(2 * HALF_ONE))
    two = odd_tables(HALF_TWO, np.arange(ROWS))
    turn = np.zeros((HALF_ONE, LANES), np.float32)
    base = (2.0 * math.pi / (2 * HALF_ONE)) * (np.arange(HALF_ONE) + 0.5)
    turn[:, 0] = np.cos(base)
    turn[:, 1] = np.cos(2 * base)
    turn[:, 2] = -np.sin(base)
    turn[:, 3] = -np.sin(2 * base)
    return (
        narrow(one),
        narrow(one[:, TAPS:].T),
        narrow(two),
        narrow(two.T),
        turn,
    )


def run(name, task):
    task()


def distance(offset, n_x, n_y):
    down, across = divmod(offset, n_y)
    return min(down, n_x - down) + min(across, n_y - across)


def next_two(running, steps):
    now = functools.reduce(jnp.add, running)
    later = running[0] * steps[0]
    for state, step in zip(running[1:], steps[1:]):
        later = later + state * step
    return jnp.concatenate([now, later], 0)


def split(value):
    high = value.astype(BF)
    return high, (value - high.astype(F32)).astype(BF)


def mm(left, right):
    return jnp.dot(left, right, preferred_element_type=F32)


def kernel(
    dims,
    query,
    key,
    value,
    *rest,
):
    sources, out, buffers, scratch = rest[:11], rest[11], rest[12:23], rest[23:]
    body(dims, query, key, value, sources, out, buffers, *scratch)


def body(
    dims,
    query,
    key,
    value,
    sources,
    out,
    buffers,
    key_own,
    key_halo,
    value_own,
    edge_sent,
    edge_seen,
    query_own,
    query_sent,
    query_seen,
    staged,
    value_tilde,
    query_tilde,
    tap_spec,
    key_spec,
    kernel_spec,
    long_kernel,
    powers,
    reverse,
    first_weight,
    eighth,
    mixed,
    states_own,
    states_away,
    states_seen,
    chip_state,
    chips_seen,
    before_ref,
    carry_own,
    carry_away,
    carry_seen,
    local_long,
    gated,
    query_wide,
    squares,
    row_sums,
    sums_seen,
    load_sems,
    send_sems,
    recv_sems,
    y_relay,
    x_relay,
    z_relay,
    plane_sems,
    chip_send,
    chip_recv,
):
    n_x, n_y, n_z, channels = dims
    (
        short_taps,
        medium_taps,
        residues,
        decay_rates,
        skip_gain,
        norm_gain,
        fwd_one,
        inv_one,
        fwd_two,
        inv_two,
        turn,
    ) = buffers
    half = channels // 2
    seq = lax.axis_index("seq")
    chan = lax.axis_index("chan")
    core = seq % 2
    y_pos = (seq // 2) % n_y
    x_pos = seq // (2 * n_y)
    n_seq = 2 * n_x * n_y
    right = (seq + 1) % n_seq
    left = (seq + n_seq - 1) % n_seq
    other = seq + 1 - 2 * core

    def along_y(step):
        return (x_pos * n_y + (y_pos + step) % n_y) * 2 + core

    def along_z(step):
        return {"chan": (chan + step) % n_z}

    def lanes(start, size):
        return pl.ds(pl.multiple_of(start, size), size)

    def along_x(step):
        return (((x_pos + step) % n_x) * n_y + y_pos) * 2 + core

    pairs = [(sources[3], decay_rates), (key, key_own), (value, value_own), (query, query_own)]
    pairs += [(sources[n], buffers[n]) for n in (6, 1, 0, 10, 2, 8, 7, 9, 4, 5)]
    loads = [
        pltpu.make_async_copy(source, target, load_sems.at[number])
        for number, (source, target) in enumerate(pairs)
    ]
    for load in loads:
        load.start()

    barrier = pltpu.get_barrier_semaphore()
    near = [{"seq": right}, {"seq": left}, {"seq": other}]
    near += [{"seq": along_y(1)}, {"seq": along_y(n_y - 1)}]
    near += [{"seq": along_x(1)}, {"seq": along_x(n_x - 1)}]
    near += [along_z(1), along_z(n_z - 1)]
    for partner in near:
        pl.semaphore_signal(barrier, inc=1, device_id=partner, device_id_type=MESH)

    sub = lax.broadcasted_iota(jnp.int32, (8, LANES), 0).astype(F32)
    loads[0].wait()

    def pole_powers(group, _):
        cols = lanes(group * LANES, LANES)
        for pole in range(POLES):
            rate = decay_rates[pl.ds(pole, 1), cols]
            powers[pole, :, cols] = jnp.exp(-rate * sub)
            reverse[pole, :, cols] = jnp.exp(-rate * (7.0 - sub))
            eighth[pole, :, cols] = jnp.broadcast_to(jnp.exp(-8.0 * rate), (8, LANES))
        return 0

    run("powers", lambda: lax.fori_loop(0, channels // LANES, pole_powers, 0))
    pl.semaphore_wait(barrier, len(near))

    def relay(sems, along, size, step):
        for way, sign in enumerate((1, size - 1)):
            pl.semaphore_signal(
                sems.at[step - 2, way], inc=1, device_id=along(sign), device_id_type=MESH
            )

    def relayed(sems, step):
        for way in range(2):
            pl.semaphore_wait(sems.at[step - 2, way], 1)

    def seq_y(step):
        return {"seq": along_y(step)}

    def seq_x(step):
        return {"seq": along_x(step)}

    def chip(position):
        return {"seq": position * 2 + core}

    if n_y > 3:
        relay(y_relay, seq_y, n_y, 2)
    if n_x > 3:
        relay(x_relay, seq_x, n_x, 2)
    if n_z > 3:
        relay(z_relay, along_z, n_z, 2)

    sent = []

    def send(source, target, where):
        number = len(sent)
        copy = pltpu.make_async_remote_copy(
            src_ref=source,
            dst_ref=target,
            send_sem=send_sems.at[number],
            recv_sem=recv_sems.at[number],
            device_id=where,
            device_id_type=MESH,
        )
        copy.start()
        sent.append(copy)
        return copy

    tiles = channels // TILE
    half_tiles = half // TILE
    half_groups = half // LANES

    def chunk(side, number):
        return (side if number < half_tiles else 1 - side) * half_tiles + number % half_tiles

    def last_rows(source, end, count):
        return source[end - EDGE : end, :].astype(F32)[EDGE - count :]

    key_copies = []

    def send_chunk():
        number = len(key_copies)
        piece = key.at[pl.ds(ROWS - TAPS, TAPS), lanes(chunk(core, number) * TILE, TILE)]
        key_copies.append(send(piece, key_halo.at[number], {"seq": right}))

    send_chunk()
    for load in loads[1:4]:
        load.wait()
    edge_sent[0:2, :] = last_rows(value_own, ROWS, 2)
    edge_sent[2:3, :] = last_rows(key_own, ROWS - TAPS, 1)
    edge_sent[3:4, :] = jnp.zeros((1, channels), F32)
    query_sent[...] = last_rows(query_own, ROWS, 2)
    edge_copy = send(edge_sent, edge_seen, {"seq": right})
    for load in loads[4:8]:
        load.wait()

    def before_halo(tile, _):
        cols = lanes(tile * TILE, TILE)
        taps = medium_taps[:, cols]
        spec = mm(fwd_one[:, :TAPS], taps)
        first = short_taps[1, :, cols].astype(F32)
        s_re = first[0:1] + first[1:2] * turn[:, 0:1] + first[2:3] * turn[:, 1:2]
        s_im = first[1:2] * turn[:, 2:3] + first[2:3] * turn[:, 3:4]
        m_re, m_im = spec[:HALF_ONE], spec[HALF_ONE:]
        scale = 1.0 / HALF_ONE
        tap_spec[:HALF_ONE, cols] = (m_re * s_re - m_im * s_im) * scale
        tap_spec[HALF_ONE:, cols] = (m_re * s_im + m_im * s_re) * scale
        key_spec[:, cols] = mm(fwd_one[:, TAPS:], key_own[:, cols])
        return 0

    def before_half(number):
        run(
            "before",
            lambda: lax.fori_loop(
                number * half_tiles, (number + 1) * half_tiles, before_halo, 0, unroll=True
            ),
        )

    before_half(0)
    send_chunk()
    before_half(1)
    send_chunk()

    def short_conv(source, halo, taps_row, target, count, first=0, last=tiles):
        def one(tile, _):
            cols = lanes(tile * TILE, TILE)
            staged[0:EDGE, :] = jnp.zeros((EDGE, TILE), F32)
            if halo is not None:
                staged[EDGE - 2 : EDGE, :] = halo[0:2, cols]
            staged[EDGE : EDGE + count, :] = source[0:count, cols].astype(F32)
            weights = short_taps[taps_row, :, cols].astype(F32)
            total = (
                weights[0:1] * staged[EDGE : EDGE + count, :]
                + weights[1:2] * staged[EDGE - 1 : EDGE - 1 + count, :]
                + weights[2:3] * staged[EDGE - 2 : EDGE - 2 + count, :]
            )
            target[0:count, cols] = total.astype(BF)
            return 0

        lax.fori_loop(first, last, one, 0)

    run("value", lambda: short_conv(value_own, None, 2, value_tilde, ROWS))
    while len(key_copies) < tiles:
        send_chunk()
    query_copy = send(query_sent, query_seen, {"seq": right})

    if n_y > 3:
        relayed(y_relay, 2)
    if n_x > 3:
        relayed(x_relay, 2)
    for step in range(1, n_x):
        pl.semaphore_signal(
            plane_sems.at[step - 1], inc=1, device_id=seq_x(step), device_id_type=MESH
        )

    loads[8].wait()

    def pole_kernel(group, _):
        cols = lanes(group * LANES, LANES)
        steps = [eighth[pole, :, cols] for pole in range(POLES)]
        start = [residues[pl.ds(pole, 1), cols] * powers[pole, :, cols] for pole in range(POLES)]
        twice = [step * step for step in steps]

        def rows(number, running):
            at = pl.ds(pl.multiple_of(number * 16, 16), 16)
            long_kernel[at, cols] = next_two(running, steps)
            return tuple(r * s for r, s in zip(running, twice))

        lax.fori_loop(0, ROWS // 16, rows, tuple(start), unroll=4)
        return 0

    first_weight[...] = residues[...] * jnp.exp(-decay_rates[...])
    run("kernel", lambda: lax.fori_loop(0, channels // LANES, pole_kernel, 0))

    for load in loads[9:]:
        load.wait()
    if n_z > 5:
        relayed(z_relay, 2)
        relay(z_relay, along_z, n_z, 3)

    def medium(number, tile):
        cols = lanes(tile * TILE, TILE)
        spec = key_spec[:, cols] + mm(fwd_one[:, :TAPS], key_halo[number])
        x_re, x_im = spec[:HALF_ONE], spec[HALF_ONE:]
        t_re, t_im = tap_spec[:HALF_ONE, cols], tap_spec[HALF_ONE:, cols]
        re, im = x_re * t_re - x_im * t_im, x_re * t_im + x_im * t_re
        key_hat = mm(inv_one[...], jnp.concatenate([re.astype(BF), im.astype(BF)], 0))
        last = short_taps[1, 2:3, cols].astype(F32) * medium_taps[TAPS - EDGE :, cols].astype(F32)[
            EDGE - 1 :
        ]
        ends = (
            edge_seen[2:3, cols]
            + key_own[ROWS - EDGE :, cols].astype(F32)[EDGE - 1 :]
        )
        row = lax.broadcasted_iota(jnp.int32, (ROWS, TILE), 0)
        key_hat = key_hat + jnp.where(row == 0, last * ends, 0.0)
        mixed[:, cols] = (key_hat * value_tilde[:, cols].astype(F32)).astype(BF)

    def end_states(group, target, target_group):
        cols = lanes(group * LANES, LANES)
        steps = [eighth[pole, :, cols] for pole in range(POLES)]

        def rows(number, running):
            block = mixed[pl.ds(pl.multiple_of(number * 16, 16), 16), cols].astype(F32)
            running = [r * s + block[:8] for r, s in zip(running, steps)]
            return tuple(r * s + block[8:] for r, s in zip(running, steps))

        empty = tuple(jnp.zeros((8, LANES), F32) for _ in range(POLES))
        running = lax.fori_loop(0, ROWS // 16, rows, empty, unroll=2)
        to = lanes(target_group * LANES, LANES)
        for pole in range(POLES):
            weighted = running[pole] * reverse[pole, :, cols]
            target[pl.ds(pole, 1), to] = jnp.sum(weighted, axis=0, keepdims=True)

    def medium_chunk(number, target):
        key_copies[number].wait_recv()

        @pl.when(seq == 0)
        def _():
            key_halo[number] = jnp.zeros((TAPS, TILE), BF)

        if number == 0:
            edge_copy.wait_recv()

            @pl.when(seq == 0)
            def _():
                edge_seen[...] = jnp.zeros_like(edge_seen)

            short_conv(value_own, edge_seen, 2, value_tilde, EDGE)
        tile = chunk(1 - core, number)
        groups = TILE // LANES

        def state_group(n, _):
            end_states(tile * groups + n, target, number % half_tiles * groups + n)
            return 0

        run("medium", lambda: medium(number, tile))
        run("states", lambda: lax.fori_loop(0, groups, state_group, 0))

    for number in range(half_tiles):
        medium_chunk(number, states_away)
    states_copy = send(states_away, states_seen, {"seq": other})
    for number in range(half_tiles, tiles):
        medium_chunk(number, states_own)

    for step in range(3, n_z // 2):
        relayed(z_relay, step)
        relay(z_relay, along_z, n_z, step + 1)

    own_cols = lanes(core * half, half)
    rates = decay_rates[:, own_cols]
    block_decay = jnp.exp(-float(ROWS) * rates)
    states_copy.wait_recv()
    mine, theirs = states_own[...], states_seen[...]
    first = jnp.where(core == 0, mine, theirs)
    second = jnp.where(core == 0, theirs, mine)
    chip_state[...] = (block_decay * first + second).astype(BF)
    for step in range(1, n_x):
        pl.semaphore_wait(plane_sems.at[step - 1], 1)
    n_chips = n_x * n_y
    position = seq // 2
    offsets = sorted(range(1, n_chips), key=lambda n: -distance(n, n_x, n_y))
    chip_copies = []
    for offset in offsets:
        copy = pltpu.make_async_remote_copy(
            src_ref=chip_state,
            dst_ref=chips_seen.at[position],
            send_sem=chip_send.at[offset],
            recv_sem=chip_recv.at[position],
            device_id=chip(lax.rem(position + offset, n_chips)),
            device_id_type=MESH,
        )
        pl.when(position + offset < n_chips)(copy.start)
        chip_copies.append((offset, copy))

    def long_local(tile, _):
        cols = lanes(tile * TILE, TILE)
        signal = mixed[:, cols]
        spec = mm(fwd_two[...], signal)
        x_re, x_im = spec[:HALF_TWO], spec[HALF_TWO:]
        k_re, k_im = kernel_spec[:HALF_TWO, cols], kernel_spec[HALF_TWO:, cols]
        re, im = x_re * k_re - x_im * k_im, x_re * k_im + x_im * k_re
        local_long[:, cols] = mm(inv_two[...], jnp.concatenate([re.astype(BF), im.astype(BF)], 0))
        return 0

    def kernel_spectrum(tile, _):
        cols = lanes(tile * TILE, TILE)
        high, low = split(long_kernel[:, cols])
        spec = mm(fwd_two[...], high) + mm(fwd_two[...], low)
        kernel_spec[:, cols] = spec * (1.0 / HALF_TWO)
        return 0

    def pregate(group, _):
        cols = lanes(group * LANES, LANES)
        long_part = local_long[:, cols] + skip_gain[:, cols] * mixed[:, cols].astype(F32)
        wide = query_tilde[:, cols].astype(F32)
        query_wide[:, cols] = wide
        gated[:, cols] = wide * long_part
        return 0

    run("kspec", lambda: lax.fori_loop(0, tiles, kernel_spectrum, 0, unroll=True))
    run("long1", lambda: lax.fori_loop(0, tiles // 2, long_local, 0, unroll=True))

    run("long2", lambda: lax.fori_loop(tiles // 2, tiles, long_local, 0, unroll=True))
    query_copy.wait_recv()

    @pl.when(seq == 0)
    def _():
        query_seen[...] = jnp.zeros_like(query_seen)

    run("query", lambda: short_conv(query_own, query_seen, 0, query_tilde, ROWS))
    run("pregate", lambda: lax.fori_loop(0, channels // LANES, pregate, 0))
    squares[...] = jnp.zeros_like(squares)

    chip_decay = jnp.exp(-float(2 * ROWS) * rates)
    before_ref[...] = jnp.zeros_like(before_ref)
    for source in range(n_chips - 1):

        @pl.when(source < position)
        def _():
            pltpu.make_async_remote_copy(
                src_ref=chip_state,
                dst_ref=chips_seen.at[source],
                send_sem=chip_send.at[0],
                recv_sem=chip_recv.at[source],
                device_id=chip(position),
                device_id_type=MESH,
            ).wait_recv()
            before_ref[...] = before_ref[...] * chip_decay + chips_seen[source].astype(F32)

    before = before_ref[...]
    after = block_decay * before + first
    carry_own[...] = jnp.where(core == 0, before, after)
    carry_away[...] = jnp.where(core == 0, after, before)
    carry_copy = send(carry_away, carry_seen, {"seq": other})


    def gate(group, carry, carry_group):
        cols = lanes(group * LANES, LANES)
        of = lanes(carry_group * LANES, LANES)
        steps = [eighth[pole, :, cols] for pole in range(POLES)]
        weight = first_weight[:, cols] * carry[:, of]
        start = [weight[pole : pole + 1] * powers[pole, :, cols] for pole in range(POLES)]
        twice = [step * step for step in steps]

        def rows(number, running):
            at = pl.ds(pl.multiple_of(number * 16, 16), 16)
            total = gated[at, cols] + query_wide[at, cols] * next_two(running, steps)
            gated[at, cols] = total
            squares[at, :] += total * total
            return tuple(r * s for r, s in zip(running, twice))

        lax.fori_loop(0, ROWS // 16, rows, tuple(start), unroll=4)

    def gate_half(side, carry):
        def one(n, _):
            gate(side * half_groups + n, carry, n)
            return 0

        run("gate", lambda: lax.fori_loop(0, half_groups, one, 0))

    gate_half(core, carry_own)
    carry_copy.wait_recv()
    gate_half(1 - core, carry_seen)

    row_sums[...] = jnp.sum(jnp.transpose(squares[...]), axis=0, keepdims=True)
    if n_z > 3:
        relayed(z_relay, n_z // 2)
    sum_copies = [
        send(row_sums, sums_seen.at[step - 1], along_z(step)) for step in range(1, n_z)
    ]
    total = row_sums[...]
    for step in range(1, n_z):
        sum_copies[step - 1].wait_recv()
        total = total + sums_seen[step - 1]
    scale = lax.rsqrt(total * (1.0 / (channels * n_z)) + 1e-05)
    scale = jnp.transpose(jnp.broadcast_to(scale, (LANES, ROWS)))

    def finish(group, _):
        cols = lanes(group * LANES, LANES)
        out[:, cols] = (gated[:, cols] * scale * norm_gain[:, cols]).astype(BF)
        return 0

    run("finish", lambda: lax.fori_loop(0, channels // LANES, finish, 0))
    for copy in sent:
        copy.wait_send()
    for offset, copy in chip_copies:
        pl.when(position + offset < n_chips)(copy.wait_send)


def solution(mesh):
    n_seq, n_z = mesh.shape["seq"], mesh.shape["chan"]
    n_y = math.isqrt(n_seq // 2)
    n_x = n_seq // 2 // n_y
    tables = make_tables()

    def local(query, key, value, short_taps, medium_taps, residues, decay_rates, skip, gain):
        channels = query.shape[1]
        half = channels // 2
        operands = (
            query,
            key,
            value,
            short_taps,
            medium_taps,
            residues,
            decay_rates,
            skip.reshape(1, channels),
            gain.reshape(1, channels),
            *(jnp.asarray(table) for table in tables),
        )
        tiles = channels // TILE
        n_copies = tiles + 2 + 1 + 1 + (n_z - 1)
        vmem = pltpu.VMEM
        scratch = [
            vmem((ROWS, channels), BF),
            vmem((tiles, TAPS, TILE), BF),
            vmem((ROWS, channels), BF),
            vmem((4, channels), F32),
            vmem((4, channels), F32),
            vmem((ROWS, channels), BF),
            vmem((2, channels), F32),
            vmem((2, channels), F32),
            vmem((EDGE + ROWS, TILE), F32),
            vmem((ROWS, channels), BF),
            vmem((ROWS, channels), BF),
            vmem((2 * HALF_ONE, channels), F32),
            vmem((2 * HALF_ONE, channels), F32),
            vmem((2 * HALF_TWO, channels), F32),
            vmem((ROWS, channels), F32),
            vmem((POLES, 8, channels), F32),
            vmem((POLES, 8, channels), F32),
            vmem((POLES, channels), F32),
            vmem((POLES, 8, channels), F32),
            vmem((ROWS, channels), BF),
            vmem((POLES, half), F32),
            vmem((POLES, half), F32),
            vmem((POLES, half), F32),
            vmem((POLES, half), BF),
            vmem((n_x * n_y, POLES, half), BF),
            vmem((POLES, half), F32),
            vmem((POLES, half), F32),
            vmem((POLES, half), F32),
            vmem((POLES, half), F32),
            vmem((ROWS, channels), F32),
            vmem((ROWS, channels), F32),
            vmem((ROWS, channels), F32),
            vmem((ROWS, LANES), F32),
            vmem((1, ROWS), F32),
            vmem((n_z - 1, 1, ROWS), F32),
            pltpu.SemaphoreType.DMA((len(operands),)),
            pltpu.SemaphoreType.DMA((n_copies,)),
            pltpu.SemaphoreType.DMA((n_copies,)),
            *(
                pltpu.SemaphoreType.REGULAR((max(1, size // 2 - 1), 2))
                for size in (n_y, n_x, n_z)
            ),
            pltpu.SemaphoreType.REGULAR((n_x,)),
            pltpu.SemaphoreType.DMA((n_x * n_y,)),
            pltpu.SemaphoreType.DMA((n_x * n_y,)),
        ]
        in_hbm = pl.BlockSpec(memory_space=pltpu.HBM)
        call = pl.pallas_call(
            functools.partial(kernel, (n_x, n_y, n_z, channels)),
            out_shape=pltpu.VMEM((ROWS, channels), BF),
            in_specs=[in_hbm] * len(operands),
            out_specs=pl.BlockSpec(memory_space=pltpu.VMEM),
            scratch_shapes=[vmem(x.shape, x.dtype) for x in operands[3:]] + scratch,
            compiler_params=pltpu.CompilerParams(
                collective_id=0, has_side_effects=True, vmem_limit_bytes=60 * 1024 * 1024
            ),
        )
        return call(*(pltpu.with_memory_space_constraint(x, pltpu.HBM) for x in operands))

    in_specs = (
        P("seq", "chan"),
        P("seq", "chan"),
        P("seq", "chan"),
        P(None, None, "chan"),
        P(None, "chan"),
        P(None, "chan"),
        P(None, "chan"),
        P("chan"),
        P("chan"),
    )
    return jax.shard_map(
        local, mesh=mesh, in_specs=in_specs, out_specs=P("seq", "chan"), check_vma=False
    )
```
